256 devices in a mesh: blk: 32 (over z, y_hi, core), bulk: 8 (over x, y_lo).
Axes of the slice: x: 4, y: 4 (y_hi: 2, y_lo: 2; y = y_hi * 2 + y_lo), z: 8, core: 2. Of those that a mesh axis runs over, the one named last changes fastest.
Arguments:
- footage_embeds: bfloat16 [32768, 768], P(('blk', 'bulk')), may hold values from -0.21582031 to 0.21582031
- caption_embeds: bfloat16 [32768, 768], P(('blk', 'bulk')), may hold values from -0.21582031 to 0.21582031
- score_scale: float32 [1], replicated, may hold values from 4 to 16
- score_offset: float32 [1], replicated, may hold values from -4 to -2
Outputs:
- video_grad: float32 [32768, 768], P(('blk', 'bulk'))
- text_grad: float32 [32768, 768], P(('blk', 'bulk'))
The draws below stay inside these ranges and needn't reach their ends.
All inputs are finite; a program needn't handle non-finite values.
Results may differ from the reference program's by a relative error of at most 0.007.
Values may be sent and summed in bfloat16 or wider, within the bound.
No kernel may reach another device: no remote copies, remote signals or barrier semaphores. Data moves between devices by JAX's collectives and lax.ppermute only.
A program may use at most 64 MiB of HBM per device.

```python
import math
import jax
import jax.numpy as jnp
from jax import lax

D = 768
GROUP = 1024
CLIPS = 32768
N_BLK = 32


def level_of(key, extent, cuts, least, high):
    gain, own = 1.0, jax.random.fold_in(key, 6)
    for dim, blocks in cuts:
        steps = jnp.exp(jax.random.uniform(jax.random.fold_in(own, dim), (blocks,), jnp.float32, least / len(cuts), high / len(cuts)))
        gain = gain * jnp.repeat(steps, extent[dim] // blocks).reshape([-1 if axis == dim else 1 for axis in range(len(extent))])
    return gain


def gaussian(stream_key, dims, width, most, shards=(), kind=jnp.bfloat16):
    entries = width * jax.random.normal(stream_key, dims, jnp.float32)
    if shards:
        entries = entries * level_of(stream_key, dims, shards, -0.22, 0.18)
    return jnp.clip(entries, -most, most).astype(kind)


def setup_inputs(seed: int = 0) -> dict:
    key_list = jax.random.split(jax.random.key(seed), 5)
    footage_embeds = gaussian(key_list[0], (CLIPS, D), 0.036, 0.21582031, ((0, 256),))
    caption_embeds = gaussian(key_list[1], (CLIPS, D), 0.036, 0.21582031, ((0, 256),))
    score_scale = jnp.clip(jnp.exp(jax.random.uniform(key_list[2], (1,), jnp.float32, math.log(4.0), math.log(16.0))), 4.0, 16.0)
    score_offset = jnp.clip(jax.random.uniform(key_list[3], (1,), jnp.float32, -4.0, -2.0), -4.0, -2.0)
    return {"footage_embeds": footage_embeds, "caption_embeds": caption_embeds, "score_scale": score_scale, "score_offset": score_offset}


EPSILON = 1e-06

def unit_rows(embedding):
    values = embedding.astype(jnp.float32)
    inverse = lax.rsqrt(lax.optimization_barrier(jnp.sum(values * values, axis=1, keepdims=True)) + EPSILON)
    return (values * inverse, inverse)

def back_rows(unit, inverse, grad_unit):
    return (grad_unit - unit * lax.optimization_barrier(jnp.sum(unit * grad_unit, axis=1, keepdims=True))) * inverse

def reference(footage_embeds, caption_embeds, score_scale, score_offset):
    smoothing_coefficient = score_scale[0]
    shifted_bias = score_offset[0]
    video_unit, video_inverse = unit_rows(footage_embeds)
    text_unit, text_inverse = unit_rows(caption_embeds)
    video_low = lax.optimization_barrier(video_unit.astype(jnp.bfloat16)).astype(jnp.float32)
    text_low = lax.optimization_barrier(text_unit.astype(jnp.bfloat16)).astype(jnp.float32)
    text_stack = text_low.reshape(N_BLK, GROUP, D)
    reach = N_BLK // 4
    band = 2 * reach + 1
    inner_ids = jnp.arange(GROUP, dtype=jnp.int32)
    highest_precision = lax.Precision.HIGHEST

    def one_block(text_grad_stack, index):
        owners = ((index - reach + jnp.arange(band, dtype=jnp.int32)) % N_BLK).astype(jnp.int32)
        column_span = jnp.take(text_stack, owners, axis=0).reshape(band * GROUP, D)
        column_ids = (owners[:, None] * GROUP + inner_ids[None, :]).reshape(band * GROUP)
        row_block_span = lax.dynamic_slice_in_dim(video_low, (index * GROUP).astype(jnp.int32), GROUP, 0)
        logit_matrix = smoothing_coefficient * jnp.dot(row_block_span, column_span.T, precision=highest_precision) + shifted_bias
        row_ids = index * GROUP + inner_ids
        label = (row_ids[:, None] == column_ids[None, :]).astype(jnp.float32)
        pair_weight = lax.optimization_barrier((jax.nn.sigmoid(logit_matrix) - label).astype(jnp.bfloat16)).astype(jnp.float32)
        video_block_rows = smoothing_coefficient * jnp.dot(pair_weight, column_span, precision=highest_precision)
        text_portion = smoothing_coefficient * jnp.dot(pair_weight.T, row_block_span, precision=highest_precision)
        text_grad_stack = text_grad_stack.at[owners].add(text_portion.reshape(band, GROUP, D))
        return (text_grad_stack, video_block_rows)
    start = jnp.zeros((N_BLK, GROUP, D), jnp.float32)
    text_grad_stack, video_blocks = lax.scan(one_block, start, jnp.arange(N_BLK, dtype=jnp.int32))
    video_grad_unit = video_blocks.reshape(CLIPS, D)
    caption_derivative_normed = text_grad_stack.reshape(CLIPS, D)
    video_grad = back_rows(video_unit, video_inverse, video_grad_unit)
    text_grad = back_rows(text_unit, text_inverse, caption_derivative_normed)
    return (video_grad, text_grad)
```

```python
import jax
import jax.numpy as jnp
from jax import lax
from jax.experimental import pallas as pl
from jax.experimental.pallas import tpu as pltpu
from jax.sharding import PartitionSpec as P

EPSILON = 1e-06
NZ, NX = 8, 4
AXES = ("blk", "bulk")
ANY = pl.BlockSpec(memory_space=pl.ANY)
SMEM = pl.BlockSpec(memory_space=pltpu.SMEM)


def move(block, x=0, z=0, y_lo=0, y_hi=0, core=0):
    pairs = []
    for blk in range(4 * NZ):
        for bulk in range(2 * NX):
            to_z = (blk // 4 + z) % NZ
            to_x = (bulk // 2 + x) % NX
            to_blk = to_z * 4 + (((blk // 2) % 2) ^ y_hi) * 2 + ((blk % 2) ^ core)
            to_bulk = to_x * 2 + ((bulk % 2) ^ y_lo)
            pairs.append((blk * 2 * NX + bulk, to_blk * 2 * NX + to_bulk))
    return lax.ppermute(block, AXES, pairs)


def add(*parts):
    total = parts[0].astype(jnp.float32)
    for part in parts[1:]:
        total = total + part.astype(jnp.float32)
    return total.astype(jnp.bfloat16)


def unit_rows(embedding):
    values = embedding.astype(jnp.float32)
    inverse = lax.rsqrt(jnp.sum(values * values, axis=1, keepdims=True) + EPSILON)
    return values * inverse, inverse


def unit_kernel(video_ref, text_ref, video_out, text_out):
    text_out[...] = unit_rows(text_ref[...])[0].astype(jnp.bfloat16)
    video_out[...] = unit_rows(video_ref[...])[0].astype(jnp.bfloat16)


def unit_low(video, text):
    shape = jax.ShapeDtypeStruct(video.shape, jnp.bfloat16)
    return pl.pallas_call(unit_kernel, out_shape=(shape, shape), name="unit_low")(video, text)


def back_kernel(scale_ref, embedding_ref, *refs):
    *parts, out = refs
    rows = out.shape[0]
    total = parts[0][:rows, :].astype(jnp.float32)
    for part in parts[1:]:
        total = total + part[:rows, :].astype(jnp.float32)
    grad_unit = scale_ref[0] * total
    unit, inverse = unit_rows(embedding_ref[...])
    along = jnp.sum(unit * grad_unit, axis=1, keepdims=True)
    out[...] = (grad_unit - unit * along) * inverse


def back_rows(scale, embedding, parts):
    vmem = pl.BlockSpec(memory_space=pltpu.VMEM)
    return pl.pallas_call(
        back_kernel,
        out_shape=jax.ShapeDtypeStruct(embedding.shape, jnp.float32),
        in_specs=[SMEM] + [vmem] * (1 + len(parts)),
        out_specs=vmem,
        name="back_rows",
    )(scale, embedding, *parts)


PAIR, D = 256, 768
N_TEXT, N_VIDEO = 5, 8
LOG2_E = 1.4426950408889634


def weight_kernel(scale_ref, offset_ref, place_ref, *refs):
    texts, videos = refs[:N_TEXT], refs[N_TEXT : N_TEXT + N_VIDEO]
    refs = refs[N_TEXT + N_VIDEO :]
    weights, video_outs, (text, video, grads) = refs[0], refs[1 : 1 + N_VIDEO], refs[1 + N_VIDEO :]
    core, y_hi = place_ref[0], place_ref[1]
    factor = -LOG2_E * scale_ref[0]
    shift = -LOG2_E * offset_ref[0]
    for i, block in enumerate(texts):
        text[pl.ds(i * PAIR, PAIR), :] = block[...]
    for i, block in enumerate(videos):
        video[pl.ds(i * PAIR, PAIR), :] = block[...]
    tile = 2 * PAIR
    steps = N_VIDEO // 2
    row = lax.broadcasted_iota(jnp.int32, (tile, PAIR), 0)
    column = lax.broadcasted_iota(jnp.int32, (tile, PAIR), 1)
    same = (row == column) & (row < PAIR // 2)
    half = lax.broadcasted_iota(jnp.int32, (1, PAIR), 1) < PAIR // 2

    @pl.loop(0, steps)
    def _(step):
        rows = pl.ds(pl.multiple_of(step * tile, tile), tile)
        video_tile = video[rows, :]
        own = step < steps // 2
        below = jnp.where(half, jnp.where(own | (core == 1), 1.0, 0.0), jnp.where(y_hi == 0, 1.0, 0.0))
        above = jnp.where(half, jnp.where(own | (core == 0), 1.0, 0.0), jnp.where(y_hi == 1, 1.0, 0.0))
        for i in range(N_TEXT):
            products = lax.dot_general(
                video_tile,
                text[pl.ds(i * PAIR, PAIR), :],
                (((1,), (1,)), ((), ())),
                preferred_element_type=jnp.float32,
            )
            weight = pl.reciprocal(1.0 + jnp.exp2(products * factor + shift), approx=True)
            if i == 0:
                weight = weight - jnp.where(same, jnp.where(step == 0, 1.0, 0.0), 0.0)
            elif i == 3:
                weight = weight * below
            elif i == 4:
                weight = weight * above
            weights[rows, pl.ds(i * PAIR, PAIR)] = weight.astype(jnp.bfloat16)
        grads[rows, :] = jnp.dot(
            weights[rows, :], text[...], preferred_element_type=jnp.float32
        ).astype(jnp.bfloat16)

    for i, block in enumerate(video_outs):
        block[...] = grads[pl.ds(i * PAIR, PAIR), :]


def text_kernel(weights, *refs):
    videos, outs, video = refs[:N_VIDEO], refs[N_VIDEO : N_VIDEO + N_TEXT], refs[N_VIDEO + N_TEXT]
    for i, block in enumerate(videos):
        video[pl.ds(i * PAIR, PAIR), :] = block[...]
    for i, block in enumerate(outs):
        block[...] = lax.dot_general(
            weights[:, pl.ds(i * PAIR, PAIR)],
            video[...],
            (((0,), (0,)), ((), ())),
            preferred_element_type=jnp.float32,
        ).astype(jnp.bfloat16)


VMEM = pl.BlockSpec(memory_space=pltpu.VMEM)
MIB = 1024 * 1024
FLOPS = 2 * N_VIDEO * N_TEXT * PAIR * PAIR * D
pair_shape = jax.ShapeDtypeStruct((PAIR, D), jnp.bfloat16)


def weights_and_video_grads(scale, offset, place, texts, videos):
    weights, *grads = pl.pallas_call(
        weight_kernel,
        out_shape=[jax.ShapeDtypeStruct((N_VIDEO * PAIR, N_TEXT * PAIR), jnp.bfloat16)]
        + [pair_shape] * N_VIDEO,
        in_specs=[SMEM] * 3 + [VMEM] * (N_TEXT + N_VIDEO),
        out_specs=[VMEM] * (1 + N_VIDEO),
        scratch_shapes=[
            pltpu.VMEM((N_TEXT * PAIR, D), jnp.bfloat16),
            pltpu.VMEM((N_VIDEO * PAIR, D), jnp.bfloat16),
            pltpu.VMEM((N_VIDEO * PAIR, D), jnp.bfloat16),
        ],
        compiler_params=pltpu.CompilerParams(vmem_limit_bytes=28 * MIB),
        cost_estimate=pl.CostEstimate(
            flops=2 * FLOPS, bytes_accessed=0, transcendentals=2 * N_VIDEO * N_TEXT * PAIR * PAIR
        ),
        name="weights_and_video_grads",
    )(scale, offset, place, *texts, *videos)
    return weights, grads


def text_grads(weights, videos):
    return pl.pallas_call(
        text_kernel,
        out_shape=[pair_shape] * N_TEXT,
        in_specs=[VMEM] * (1 + N_VIDEO),
        out_specs=[VMEM] * N_TEXT,
        scratch_shapes=[pltpu.VMEM((N_VIDEO * PAIR, D), jnp.bfloat16)],
        compiler_params=pltpu.CompilerParams(vmem_limit_bytes=20 * MIB),
        cost_estimate=pl.CostEstimate(flops=FLOPS, bytes_accessed=0, transcendentals=0),
        name="text_grads",
    )(weights, *videos)


def local(footage_embeds, caption_embeds, score_scale, score_offset):
    blk = lax.axis_index("blk")
    place = jnp.stack([blk % 2, (blk // 2) % 2]).astype(jnp.int32)
    rows = footage_embeds.shape[0]
    v0, t0 = unit_low(footage_embeds, caption_embeds)

    tp, v1 = move(t0, y_hi=1), move(v0, y_lo=1)
    a1m, a1p = move(t0, z=1), move(t0, z=-1)
    v01 = jnp.concatenate([v0, v1])
    vm, vp = move(v01, x=1), move(v01, x=-1)
    b1m, b1p = move(tp, z=1), move(tp, z=-1)
    t01 = jnp.concatenate([t0, tp])
    tm, tq = jnp.concatenate([a1m, b1m]), jnp.concatenate([a1p, b1p])
    tmm, tqq = move(tm, z=1), move(tq, z=-1)
    v2 = jnp.concatenate([move(vm[:rows], x=1), move(vp[rows:], x=-1)])
    own = [v01, vm, vp, v2]
    videos = own + [move(block, core=1) for block in own]
    texts = [t01, tm, tq, tmm, tqq]

    weights, vg = weights_and_video_grads(score_scale, score_offset, place, texts, videos)
    tg = text_grads(weights, videos)

    g01, gm, gp, g2 = vg[:4]
    r01, rm, rp, r2 = [move(block, core=1) for block in vg[4:]]
    to_m = move(add(g2[:rows], r2[:rows]), x=-1)
    to_p = move(add(g2[rows:], r2[rows:]), x=1)
    none = jnp.zeros_like(to_m)
    gm = add(gm, rm, jnp.concatenate([to_m, none]))
    gp = add(gp, rp, jnp.concatenate([none, to_p]))
    from_p, from_m = move(gp, x=1), move(gm, x=-1)
    last = move(add(g01[rows:], r01[rows:], from_p[rows:], from_m[rows:]), y_lo=1)
    video_parts = [g01, r01, from_p, from_m, last]

    h01, hm, hq, hmm, hqq = tg
    hq = add(hq, move(hqq, z=1))
    hm = add(hm, move(hmm, z=-1))
    up, down = move(hq, z=1), move(hm, z=-1)
    last = move(add(h01[rows:], up[rows:], down[rows:]), y_hi=1)
    text_parts = [h01, up, down, last]

    video_grad = back_rows(score_scale, footage_embeds, video_parts)
    text_grad = back_rows(score_scale, caption_embeds, text_parts)
    return (video_grad, text_grad)


def solution(mesh):
    assert mesh.shape["blk"] == 4 * NZ and mesh.shape["bulk"] == 2 * NX
    return jax.shard_map(
        local,
        mesh=mesh,
        in_specs=(P(AXES, None), P(AXES, None), P(), P()),
        out_specs=(P(AXES, None), P(AXES, None)),
        check_vma=False,
    )
```

```python
import functools

import jax
import jax.numpy as jnp
from jax import lax
from jax.experimental import pallas as pl
from jax.experimental.pallas import tpu as pltpu
from jax.sharding import PartitionSpec as P

EPSILON = 1e-06
NZ, NX = 8, 4
AXES = ("blk", "bulk")
ANY = pl.BlockSpec(memory_space=pl.ANY)
SMEM = pl.BlockSpec(memory_space=pltpu.SMEM)


def move(block, x=0, z=0, y_lo=0, y_hi=0, core=0):
    pairs = []
    for blk in range(4 * NZ):
        for bulk in range(2 * NX):
            to_z = (blk // 4 + z) % NZ
            to_x = (bulk // 2 + x) % NX
            to_blk = to_z * 4 + (((blk // 2) % 2) ^ y_hi) * 2 + ((blk % 2) ^ core)
            to_bulk = to_x * 2 + ((bulk % 2) ^ y_lo)
            pairs.append((blk * 2 * NX + bulk, to_blk * 2 * NX + to_bulk))
    return lax.ppermute(block, AXES, pairs)


def add(*parts):
    total = parts[0].astype(jnp.float32)
    for part in parts[1:]:
        total = total + part.astype(jnp.float32)
    return total.astype(jnp.bfloat16)


def unit_rows(embedding):
    values = embedding.astype(jnp.float32)
    inverse = lax.rsqrt(jnp.sum(values * values, axis=1, keepdims=True) + EPSILON)
    return values * inverse, inverse


def unit_kernel(video_ref, text_ref, video_out, text_out):
    text_out[...] = unit_rows(text_ref[...])[0].astype(jnp.bfloat16)
    video_out[...] = unit_rows(video_ref[...])[0].astype(jnp.bfloat16)


def unit_low(video, text):
    shape = jax.ShapeDtypeStruct(video.shape, jnp.bfloat16)
    return pl.pallas_call(
        unit_kernel,
        out_shape=(shape, shape),
        compiler_params=pltpu.CompilerParams(vmem_limit_bytes=4 * 1024 * 1024),
        name="unit_low",
    )(video, text)


def back_kernel(scale_ref, embedding_ref, *refs):
    *parts, out = refs
    rows = out.shape[0]
    total = parts[0][:rows, :].astype(jnp.float32)
    for part in parts[1:]:
        total = total + part[:rows, :].astype(jnp.float32)
    grad_unit = scale_ref[0] * total
    unit, inverse = unit_rows(embedding_ref[...])
    along = jnp.sum(unit * grad_unit, axis=1, keepdims=True)
    out[...] = (grad_unit - unit * along) * inverse


def back_rows(scale, embedding, parts):
    vmem = pl.BlockSpec(memory_space=pltpu.VMEM)
    return pl.pallas_call(
        back_kernel,
        out_shape=jax.ShapeDtypeStruct(embedding.shape, jnp.float32),
        in_specs=[SMEM] + [vmem] * (1 + len(parts)),
        out_specs=vmem,
        compiler_params=pltpu.CompilerParams(vmem_limit_bytes=8 * 1024 * 1024),
        name="back_rows",
    )(scale, embedding, *parts)


PAIR, D = 256, 768
N_TEXT, N_VIDEO = 5, 8
LOG2_E = 1.4426950408889634


def put(target, blocks):
    place = 0
    for block in blocks:
        target[pl.ds(place, block.shape[0]), :] = block[...]
        place += block.shape[0]


def weigh(scale_ref, offset_ref, place_ref, weights, text, video, has_own_text):
    core, y_hi = place_ref[0], place_ref[1]
    factor = -LOG2_E * scale_ref[0]
    shift = -LOG2_E * offset_ref[0]
    tile = video.shape[0] // 2
    row = lax.broadcasted_iota(jnp.int32, (tile, PAIR), 0)
    column = lax.broadcasted_iota(jnp.int32, (tile, PAIR), 1)
    same = (row == column) & (row < PAIR // 2)
    half = lax.broadcasted_iota(jnp.int32, (1, PAIR), 1) < PAIR // 2

    @pl.loop(0, 2)
    def _(step):
        rows = pl.ds(pl.multiple_of(step * tile, tile), tile)
        video_tile = video[rows, :]
        own = step == 0
        below = jnp.where(half, jnp.where(own | (core == 1), 1.0, 0.0), jnp.where(y_hi == 0, 1.0, 0.0))
        above = jnp.where(half, jnp.where(own | (core == 0), 1.0, 0.0), jnp.where(y_hi == 1, 1.0, 0.0))
        for i in range(N_TEXT):
            products = lax.dot_general(
                video_tile,
                text[pl.ds(i * PAIR, PAIR), :],
                (((1,), (1,)), ((), ())),
                preferred_element_type=jnp.float32,
            )
            weight = pl.reciprocal(1.0 + jnp.exp2(products * factor + shift), approx=True)
            if i == 0 and has_own_text:
                weight = weight - jnp.where(same, jnp.where(own, 1.0, 0.0), 0.0)
            elif i == 3:
                weight = weight * below
            elif i == 4:
                weight = weight * above
            weights[rows, pl.ds(i * PAIR, PAIR)] = weight.astype(jnp.bfloat16)


def near_kernel(scale_ref, offset_ref, place_ref, *refs):
    texts, videos = refs[:9], refs[9:-3]
    weights, text, video = refs[-3:]
    put(text, texts[:7] + texts[8:] + texts[7:])
    put(video, videos)
    weigh(scale_ref, offset_ref, place_ref, weights, text, video, True)


def far_kernel(scale_ref, offset_ref, place_ref, text, *refs):
    *videos, weights, video = refs
    put(video, videos)
    weigh(scale_ref, offset_ref, place_ref, weights, text, video, False)


def text_kernel(first, near_weights, near_video, far_weights, far_video, *outs):
    for i, block in enumerate(outs):
        columns = pl.ds((first + i) * PAIR, PAIR)
        contract = (((0,), (0,)), ((), ()))
        near = lax.dot_general(
            near_weights[:, columns], near_video[...], contract, preferred_element_type=jnp.float32
        )
        far = lax.dot_general(
            far_weights[:, columns], far_video[...], contract, preferred_element_type=jnp.float32
        )
        block[...] = (near + far).astype(jnp.bfloat16)


def video_kernel(half, near_weights, far_weights, text, out):
    near_rows, far_rows = near_weights.shape[0] // 2, far_weights.shape[0] // 2
    for weights, rows, place in ((near_weights, near_rows, 0), (far_weights, far_rows, near_rows)):
        out[pl.ds(place, rows), :] = jnp.dot(
            weights[pl.ds(half * rows, rows), :], text[...], preferred_element_type=jnp.float32
        ).astype(jnp.bfloat16)


VMEM = pl.BlockSpec(memory_space=pltpu.VMEM)
MIB = 1024 * 1024
FLOPS = 2 * N_VIDEO * N_TEXT * PAIR * PAIR * D


def low(rows, columns=D):
    return jax.ShapeDtypeStruct((rows, columns), jnp.bfloat16)


def cost(flops, transcendentals=0):
    return pl.CostEstimate(flops=flops, bytes_accessed=0, transcendentals=transcendentals)


def near_weights(scalars, texts, videos):
    rows = sum(block.shape[0] for block in videos)
    return pl.pallas_call(
        near_kernel,
        out_shape=[low(rows, N_TEXT * PAIR), low(N_TEXT * PAIR), low(rows)],
        in_specs=[SMEM] * 3 + [VMEM] * (9 + len(videos)),
        out_specs=[VMEM] * 3,
        compiler_params=pltpu.CompilerParams(vmem_limit_bytes=20 * MIB),
        cost_estimate=cost(FLOPS * 3 // 4, 2 * rows * N_TEXT * PAIR),
        name="near_weights",
    )(*scalars, *texts, *videos)


def far_weights(scalars, text, videos):
    rows = sum(block.shape[0] for block in videos)
    return pl.pallas_call(
        far_kernel,
        out_shape=[low(rows, N_TEXT * PAIR), low(rows)],
        in_specs=[SMEM] * 3 + [VMEM] * (1 + len(videos)),
        out_specs=[VMEM] * 2,
        compiler_params=pltpu.CompilerParams(vmem_limit_bytes=12 * MIB),
        cost_estimate=cost(FLOPS // 4, 2 * rows * N_TEXT * PAIR),
        name="far_weights",
    )(*scalars, text, *videos)


def text_grads(near, near_video, far, far_video, first, count):
    return pl.pallas_call(
        functools.partial(text_kernel, first),
        out_shape=[low(PAIR)] * count,
        in_specs=[VMEM] * 4,
        out_specs=[VMEM] * count,
        compiler_params=pltpu.CompilerParams(vmem_limit_bytes=16 * MIB),
        cost_estimate=cost(FLOPS * count // N_TEXT),
        name="text_grads",
    )(near, near_video, far, far_video)


def video_grads(near, far, text, half):
    return pl.pallas_call(
        functools.partial(video_kernel, half),
        out_shape=low(N_VIDEO * PAIR // 2),
        in_specs=[VMEM] * 3,
        out_specs=VMEM,
        compiler_params=pltpu.CompilerParams(vmem_limit_bytes=16 * MIB),
        cost_estimate=cost(FLOPS // 2),
        name="video_grads",
    )(near, far, text)


def local(footage_embeds, caption_embeds, score_scale, score_offset):
    blk = lax.axis_index("blk")
    core, y_hi = blk % 2, (blk // 2) % 2
    scalars = score_scale, score_offset, jnp.stack([core, y_hi]).astype(jnp.int32)
    rows = footage_embeds.shape[0]
    v0, t0 = unit_low(footage_embeds, caption_embeds)

    tp, v1 = move(t0, y_hi=1), move(v0, y_lo=1)
    a1m, a1p = move(t0, z=1), move(t0, z=-1)
    v1, tp, a1m, a1p = lax.optimization_barrier((v1, tp, a1m, a1p))
    v01 = jnp.concatenate([v0, v1])
    vm, vp = move(v01, x=1), move(v01, x=-1)
    a2m, a2p = move(a1m, z=1), move(a1p, z=-1)
    b1m, b1p = move(tp, z=1), move(tp, z=-1)
    vm, vp, b1m, b1p, a2m, a2p = lax.optimization_barrier((vm, vp, b1m, b1p, a2m, a2p))
    b2 = move_by_y_hi(jnp.where(y_hi == 1, b1p, b1m))
    v2 = jnp.concatenate([move(vm[:rows], x=1), move(vp[rows:], x=-1)])
    own = jnp.concatenate([v01, vm, vp])
    videos = [own, move(own, core=1)]
    texts = [t0, tp, a1m, b1m, a1p, b1p, a2m, a2p, b2]

    near, text, near_video = near_weights(scalars, texts, videos)
    far, far_video = far_weights(scalars, text, [v2, move(v2, core=1)])

    hmm, hqq = text_grads(near, near_video, far, far_video, 3, 2)
    near, hmm, hqq = lax.optimization_barrier((near, hmm, hqq))
    sibling = video_grads(near, far, text, 1)
    near, sibling = lax.optimization_barrier((near, sibling))
    own = video_grads(near, far, text, 0)
    near, own = lax.optimization_barrier((near, own))
    h01, hm, hq = text_grads(near, near_video, far, far_video, 0, 3)
    hmm, hqq, other, own, h01, hm, hq = lax.optimization_barrier(
        (move(hmm, z=-1), move(hqq, z=1), move(sibling, core=1), own, h01, hm, hq)
    )

    up, down = move(add(hq, hqq), z=1), move(add(hm, hmm), z=-1)
    last = move(add(h01[rows:], up[rows:], down[rows:]), y_hi=1)
    text_parts = [h01, up, down, last]

    def total(index, *more):
        place = slice(index * rows, (index + 1) * rows)
        return add(own[place], other[place], *more)

    to_m, to_p = lax.optimization_barrier((move(total(6), x=-1), move(total(7), x=1)))
    gm = jnp.concatenate([total(2, to_m), total(3)])
    gp = jnp.concatenate([total(4), total(5, to_p)])
    from_p, from_m = move(gp, x=1), move(gm, x=-1)
    last = move(total(1, from_p[rows:], from_m[rows:]), y_lo=1)
    video_parts = [own, other, from_p, from_m, last]

    video_grad = back_rows(score_scale, footage_embeds, video_parts)
    text_grad = back_rows(score_scale, caption_embeds, text_parts)
    return (video_grad, text_grad)


def move_by_y_hi(block):
    pairs = []
    for blk in range(4 * NZ):
        step = 1 if (blk // 2) % 2 == 0 else -1
        to_blk = ((blk // 4 + step) % NZ) * 4 + blk % 4
        for bulk in range(2 * NX):
            pairs.append((blk * 2 * NX + bulk, to_blk * 2 * NX + bulk))
    return lax.ppermute(block, AXES, pairs)


def solution(mesh):
    assert mesh.shape["blk"] == 4 * NZ and mesh.shape["bulk"] == 2 * NX
    return jax.shard_map(
        local,
        mesh=mesh,
        in_specs=(P(AXES, None), P(AXES, None), P(), P()),
        out_specs=(P(AXES, None), P(AXES, None)),
        check_vma=False,
    )
```

```python
import functools

import jax
import jax.numpy as jnp
from jax import lax
from jax.experimental import pallas as pl
from jax.experimental.pallas import tpu as pltpu
from jax.sharding import PartitionSpec as P

EPSILON = 1e-06
NZ, NX = 8, 4
AXES = ("blk", "bulk")
ANY = pl.BlockSpec(memory_space=pl.ANY)
SMEM = pl.BlockSpec(memory_space=pltpu.SMEM)


def move(block, x=0, z=0, y_lo=0, y_hi=0, core=0):
    pairs = []
    for blk in range(4 * NZ):
        for bulk in range(2 * NX):
            to_z = (blk // 4 + z) % NZ
            to_x = (bulk // 2 + x) % NX
            to_blk = to_z * 4 + (((blk // 2) % 2) ^ y_hi) * 2 + ((blk % 2) ^ core)
            to_bulk = to_x * 2 + ((bulk % 2) ^ y_lo)
            pairs.append((blk * 2 * NX + bulk, to_blk * 2 * NX + to_bulk))
    return lax.ppermute(block, AXES, pairs)


def add(*parts):
    total = parts[0].astype(jnp.float32)
    for part in parts[1:]:
        total = total + part.astype(jnp.float32)
    return total.astype(jnp.bfloat16)


def unit_rows(embedding):
    values = embedding.astype(jnp.float32)
    inverse = lax.rsqrt(jnp.sum(values * values, axis=1, keepdims=True) + EPSILON)
    return values * inverse, inverse


def unit_kernel(video_ref, text_ref, video_out, text_out):
    text_out[...] = unit_rows(text_ref[...])[0].astype(jnp.bfloat16)
    video_out[...] = unit_rows(video_ref[...])[0].astype(jnp.bfloat16)


def unit_low(video, text):
    shape = jax.ShapeDtypeStruct(video.shape, jnp.bfloat16)
    return pl.pallas_call(unit_kernel, out_shape=(shape, shape), name="unit_low")(video, text)


def back_kernel(scale_ref, embedding_ref, *refs):
    *parts, out = refs
    rows = out.shape[0]
    total = parts[0][:rows, :].astype(jnp.float32)
    for part in parts[1:]:
        total = total + part[:rows, :].astype(jnp.float32)
    grad_unit = scale_ref[0] * total
    unit, inverse = unit_rows(embedding_ref[...])
    along = jnp.sum(unit * grad_unit, axis=1, keepdims=True)
    out[...] = (grad_unit - unit * along) * inverse


def back_rows(scale, embedding, parts):
    vmem = pl.BlockSpec(memory_space=pltpu.VMEM)
    return pl.pallas_call(
        back_kernel,
        out_shape=jax.ShapeDtypeStruct(embedding.shape, jnp.float32),
        in_specs=[SMEM] + [vmem] * (1 + len(parts)),
        out_specs=vmem,
        compiler_params=pltpu.CompilerParams(vmem_limit_bytes=8 * 1024 * 1024),
        name="back_rows",
    )(scale, embedding, *parts)


PAIR, D = 256, 768
N_TEXT, N_VIDEO = 5, 8
LOG2_E = 1.4426950408889634


def put(target, blocks):
    place = 0
    for block in blocks:
        target[pl.ds(place, block.shape[0]), :] = block[...]
        place += block.shape[0]


def pair_weight(scale_ref, offset_ref, video, text):
    products = lax.dot_general(
        video, text, (((1,), (1,)), ((), ())), preferred_element_type=jnp.float32
    )
    shifted = products * (-LOG2_E * scale_ref[0]) + -LOG2_E * offset_ref[0]
    return pl.reciprocal(1.0 + jnp.exp2(shifted), approx=True)


def edge_mask(core, own):
    half = lax.broadcasted_iota(jnp.int32, (1, PAIR), 1) < PAIR // 2
    below, above = own | (core == 1), own | (core == 0)
    return jnp.where(half, jnp.where(below, 1.0, 0.0), jnp.where(above, 1.0, 0.0))


def tile_rows(step, tile):
    return pl.ds(pl.multiple_of(step * tile, tile), tile)


def near_kernel(scale_ref, offset_ref, place_ref, *refs):
    texts, videos = refs[:8], refs[8:-4]
    weights, text, video, sems = refs[-4:]
    copies = []
    for target, blocks in ((text, texts), (video, videos)):
        place = 0
        for block in blocks:
            part = target.at[pl.ds(place, block.shape[0]), :]
            copies.append(pltpu.make_async_copy(block, part, sems.at[len(copies)]))
            place += block.shape[0]
    for copy in copies:
        copy.start()
    for copy in copies:
        copy.wait()
    core = place_ref[0]
    tile = video.shape[0] // 2
    row = lax.broadcasted_iota(jnp.int32, (tile, PAIR), 0)
    column = lax.broadcasted_iota(jnp.int32, (tile, PAIR), 1)
    same = (row == column) & (row < PAIR // 2)

    @pl.loop(0, 2)
    def _(step):
        rows = tile_rows(step, tile)
        video_tile = video[rows, :]
        own = step == 0
        for i in range(4):
            columns = pl.ds(i * PAIR, PAIR)
            weight = pair_weight(scale_ref, offset_ref, video_tile, text[columns, :])
            if i == 0:
                weight = weight - jnp.where(same, jnp.where(own, 1.0, 0.0), 0.0)
            elif i == 3:
                weight = weight * edge_mask(core, own)
            weights[rows, columns] = weight.astype(jnp.bfloat16)


def text_sum(*pairs):
    total = None
    for weights, video in pairs:
        part = lax.dot_general(
            weights, video[...], (((0,), (0,)), ((), ())), preferred_element_type=jnp.float32
        )
        total = part if total is None else total + part
    return total


def video_sums(half, near, last_weights, far, text, last, outs):
    def dot(a, b):
        return jnp.dot(a, b[...], preferred_element_type=jnp.float32)

    tile = near.shape[0] // 2
    rows = pl.ds(half * tile, tile)
    total = dot(near[rows, :], text) + dot(last_weights[rows, :], last)
    for i, out in enumerate(outs[:3]):
        out[...] = total[i * PAIR : (i + 1) * PAIR].astype(jnp.bfloat16)
    rows = pl.ds(half * PAIR, PAIR)
    total = dot(far[rows, : 4 * PAIR], text) + dot(far[rows, 4 * PAIR :], last)
    outs[3][...] = total.astype(jnp.bfloat16)


def far_kernel(scale_ref, offset_ref, place_ref, near, text, near_video, last, *refs):
    videos, (last_weights, weights, video, below, above, *outs) = refs[:2], refs[2:]
    put(video, videos)
    core, y_hi = place_ref[0], place_ref[1]
    near_tile, rows = near_video.shape[0] // 2, PAIR // 2

    @pl.loop(0, 2)
    def _(step):
        rows = tile_rows(step, near_tile)
        weight = pair_weight(scale_ref, offset_ref, near_video[rows, :], last[...])
        last_weights[rows, :] = weight.astype(jnp.bfloat16)
        rows = tile_rows(step, PAIR)
        video_tile = video[rows, :]
        for i in range(4):
            columns = pl.ds(i * PAIR, PAIR)
            weight = pair_weight(scale_ref, offset_ref, video_tile, text[columns, :])
            if i == 3:
                weight = weight * edge_mask(core, step == 0)
            weights[rows, columns] = weight.astype(jnp.bfloat16)
        weight = pair_weight(scale_ref, offset_ref, video_tile, last[...])
        weights[rows, pl.ds(4 * PAIR, PAIR // 2)] = weight.astype(jnp.bfloat16)

    video_sums(1, near, last_weights, weights, text, last, outs)
    columns = pl.ds(3 * PAIR, PAIR)
    edges = text_sum((near[:, columns], near_video), (weights[:, columns], video))
    columns = pl.ds(4 * PAIR, rows)
    total = text_sum((last_weights[...], near_video), (weights[:, columns], video))
    below[:rows, :] = edges[:rows].astype(jnp.bfloat16)
    above[:rows, :] = edges[rows:].astype(jnp.bfloat16)
    below[rows:, :] = (total * jnp.where(y_hi == 0, 1.0, 0.0)).astype(jnp.bfloat16)
    above[rows:, :] = (total * jnp.where(y_hi == 1, 1.0, 0.0)).astype(jnp.bfloat16)


def last_kernel(near, last_weights, far, text, last, near_video, far_video, *outs):
    video_sums(0, near, last_weights, far, text, last, outs[:4])
    for i, block in enumerate(outs[4:]):
        columns = pl.ds(i * PAIR, PAIR)
        total = text_sum((near[:, columns], near_video), (far[:, columns], far_video))
        block[...] = total.astype(jnp.bfloat16)


VMEM = pl.BlockSpec(memory_space=pltpu.VMEM)
MIB = 1024 * 1024
FLOPS = 2 * N_VIDEO * N_TEXT * PAIR * PAIR * D


def low(rows, columns=D):
    return jax.ShapeDtypeStruct((rows, columns), jnp.bfloat16)


def cost(flops, transcendentals=0):
    return pl.CostEstimate(flops=flops, bytes_accessed=0, transcendentals=transcendentals)


def call(kernel, name, scalars, arrays, outs, grant, flops, transcendentals=0, copies=0):
    return pl.pallas_call(
        kernel,
        out_shape=outs,
        in_specs=[SMEM] * len(scalars) + [ANY if copies else VMEM] * len(arrays),
        out_specs=[VMEM] * len(outs),
        scratch_shapes=[pltpu.SemaphoreType.DMA((copies,))] if copies else [],
        compiler_params=pltpu.CompilerParams(vmem_limit_bytes=grant * MIB),
        cost_estimate=cost(flops, transcendentals),
        name=name,
    )(*scalars, *arrays)


def local(footage_embeds, caption_embeds, score_scale, score_offset):
    blk = lax.axis_index("blk")
    core, y_hi = blk % 2, (blk // 2) % 2
    place = jnp.stack([core, y_hi]).astype(jnp.int32)
    scalars = [score_scale, score_offset, place]
    rows = footage_embeds.shape[0]
    v0, t0 = unit_low(footage_embeds, caption_embeds)

    tp, v1 = move(t0, y_hi=1), move(v0, y_lo=1)
    a1m, a1p = move(t0, z=1), move(t0, z=-1)
    v1, tp, a1m, a1p = lax.optimization_barrier((v1, tp, a1m, a1p))
    v01 = jnp.concatenate([v0, v1])
    vm, vp = move(v01, x=1), move(v01, x=-1)
    a2m, a2p = move(a1m, z=1), move(a1p, z=-1)
    b1m, b1p = move(tp, z=1), move(tp, z=-1)
    vm, vp, b1m, b1p, a2m, a2p = lax.optimization_barrier((vm, vp, b1m, b1p, a2m, a2p))
    b2 = move_by_y_hi(jnp.where(y_hi == 1, b1p, b1m))
    v2 = move_by_core(jnp.where(core == 1, vp, vm), 1)
    own = [v01, vm, vp]
    videos = own + [move(block, core=1) for block in own]
    texts = [t0, tp, a1m, b1m, a1p, b1p, a2m, a2p]

    near_rows, far_rows = 6 * PAIR, 2 * PAIR
    near, text, near_video = call(
        near_kernel,
        "near_weights",
        scalars,
        texts + videos,
        [low(near_rows, 4 * PAIR), low(4 * PAIR), low(near_rows)],
        20,
        FLOPS * 3 // 5,
        2 * near_rows * 4 * PAIR,
        len(texts + videos),
    )
    v2, b2, near = lax.optimization_barrier((v2, b2, near))
    last, far, far_video, hmm, hqq, s01, sm, sp, s2 = call(
        far_kernel,
        "far_weights_and_sums",
        scalars,
        [near, text, near_video, b2, v2, move(v2, core=1)],
        [low(near_rows, PAIR // 2), low(far_rows, 4 * PAIR + PAIR // 2), low(far_rows)]
        + [low(PAIR)] * 6,
        24,
        FLOPS * 5 // 4,
        2 * far_rows * 5 * PAIR,
    )

    r2 = move(s2, core=1)
    g01, gm, gp, g2, h01, hm, hq = call(
        last_kernel,
        "own_video_and_near_text_sums",
        [],
        [near, last, far, text, b2, near_video, far_video],
        [low(PAIR)] * 7,
        24,
        FLOPS,
    )
    hmm, hqq, r2, g01, gm, gp, g2, h01, hm, hq = lax.optimization_barrier(
        (move(hmm, z=-1), move(hqq, z=1), r2, g01, gm, gp, g2, h01, hm, hq)
    )

    up, down = move(add(hq, hqq), z=1), move(add(hm, hmm), z=-1)
    last = move(add(h01[rows:], up[rows:], down[rows:]), y_hi=1)
    text_parts = [h01, up, down, last]

    back = move_by_core(add(g2, r2), -1)
    r01, rm, rp = [move(block, core=1) for block in (s01, sm, sp)]
    none = jnp.zeros((), jnp.bfloat16)
    gm = add(gm, rm, jnp.where(core == 0, back, none))
    gp = add(gp, rp, jnp.where(core == 1, back, none))
    from_p, from_m = move(gp, x=1), move(gm, x=-1)
    last = move(add(g01[rows:], r01[rows:], from_p[rows:], from_m[rows:]), y_lo=1)
    video_parts = [g01, r01, from_p, from_m, last]

    video_grad = back_rows(score_scale, footage_embeds, video_parts)
    text_grad = back_rows(score_scale, caption_embeds, text_parts)
    return (video_grad, text_grad)


def move_by_core(block, sign):
    pairs = []
    for blk in range(4 * NZ):
        step = sign if blk % 2 == 0 else -sign
        for bulk in range(2 * NX):
            to_bulk = ((bulk // 2 + step) % NX) * 2 + bulk % 2
            pairs.append((blk * 2 * NX + bulk, blk * 2 * NX + to_bulk))
    return lax.ppermute(block, AXES, pairs)


def move_by_y_hi(block):
    pairs = []
    for blk in range(4 * NZ):
        step = 1 if (blk // 2) % 2 == 0 else -1
        to_blk = ((blk // 4 + step) % NZ) * 4 + blk % 4
        for bulk in range(2 * NX):
            pairs.append((blk * 2 * NX + bulk, to_blk * 2 * NX + bulk))
    return lax.ppermute(block, AXES, pairs)


def solution(mesh):
    assert mesh.shape["blk"] == 4 * NZ and mesh.shape["bulk"] == 2 * NX
    return jax.shard_map(
        local,
        mesh=mesh,
        in_specs=(P(AXES, None), P(AXES, None), P(), P()),
        out_specs=(P(AXES, None), P(AXES, None)),
        check_vma=False,
    )
```

```python
import functools

import jax
import jax.numpy as jnp
from jax import lax
from jax.experimental import pallas as pl
from jax.experimental.pallas import tpu as pltpu
from jax.sharding import PartitionSpec as P

EPSILON = 1e-06
NZ, NX = 8, 4
AXES = ("blk", "bulk")
ANY = pl.BlockSpec(memory_space=pl.ANY)
SMEM = pl.BlockSpec(memory_space=pltpu.SMEM)


def move(block, x=0, z=0, y_lo=0, y_hi=0, core=0):
    pairs = []
    for blk in range(4 * NZ):
        for bulk in range(2 * NX):
            to_z = (blk // 4 + z) % NZ
            to_x = (bulk // 2 + x) % NX
            to_blk = to_z * 4 + (((blk // 2) % 2) ^ y_hi) * 2 + ((blk % 2) ^ core)
            to_bulk = to_x * 2 + ((bulk % 2) ^ y_lo)
            pairs.append((blk * 2 * NX + bulk, to_blk * 2 * NX + to_bulk))
    return lax.ppermute(block, AXES, pairs)


def add(*parts):
    total = parts[0].astype(jnp.float32)
    for part in parts[1:]:
        total = total + part.astype(jnp.float32)
    return total.astype(jnp.bfloat16)


def unit_rows(embedding):
    values = embedding.astype(jnp.float32)
    inverse = lax.rsqrt(jnp.sum(values * values, axis=1, keepdims=True) + EPSILON)
    return values * inverse, inverse


def unit_kernel(video_ref, text_ref, video_out, text_out):
    text_out[...] = unit_rows(text_ref[...])[0].astype(jnp.bfloat16)
    video_out[...] = unit_rows(video_ref[...])[0].astype(jnp.bfloat16)


def unit_low(video, text):
    shape = pltpu.VMEM(video.shape, jnp.bfloat16)
    return pl.pallas_call(unit_kernel, out_shape=(shape, shape), name="unit_low")(video, text)


def back_kernel(scale_ref, embedding_ref, *refs):
    *parts, out = refs
    rows = out.shape[0]
    total = parts[0][:rows, :].astype(jnp.float32)
    for part in parts[1:]:
        total = total + part[:rows, :].astype(jnp.float32)
    grad_unit = scale_ref[0] * total
    unit, inverse = unit_rows(embedding_ref[...])
    along = jnp.sum(unit * grad_unit, axis=1, keepdims=True)
    out[...] = (grad_unit - unit * along) * inverse


def back_rows(scale, embedding, parts):
    vmem = pl.BlockSpec(memory_space=pltpu.VMEM)
    return pl.pallas_call(
        back_kernel,
        out_shape=jax.ShapeDtypeStruct(embedding.shape, jnp.float32),
        in_specs=[SMEM] + [vmem] * (1 + len(parts)),
        out_specs=vmem,
        compiler_params=pltpu.CompilerParams(vmem_limit_bytes=8 * 1024 * 1024),
        name="back_rows",
    )(scale, embedding, *parts)


PAIR, D = 256, 768
N_TEXT, N_VIDEO = 5, 8
LOG2_E = 1.4426950408889634


def put(target, blocks):
    place = 0
    for block in blocks:
        target[pl.ds(place, block.shape[0]), :] = block[...]
        place += block.shape[0]


def pair_weight(scale_ref, offset_ref, video, text):
    products = lax.dot_general(
        video, text, (((1,), (1,)), ((), ())), preferred_element_type=jnp.float32
    )
    shifted = products * (-LOG2_E * scale_ref[0]) + -LOG2_E * offset_ref[0]
    return pl.reciprocal(1.0 + jnp.exp2(shifted), approx=True)


def edge_mask(core, own):
    half = lax.broadcasted_iota(jnp.int32, (1, PAIR), 1) < PAIR // 2
    below, above = own | (core == 1), own | (core == 0)
    return jnp.where(half, jnp.where(below, 1.0, 0.0), jnp.where(above, 1.0, 0.0))


def tile_rows(step, tile):
    return pl.ds(pl.multiple_of(step * tile, tile), tile)


def near_kernel(scale_ref, offset_ref, place_ref, *refs):
    texts, videos = refs[:8], refs[8:-4]
    weights, text, video, sems = refs[-4:]
    copies = []
    for target, blocks in ((text, texts), (video, videos)):
        place = 0
        for block in blocks:
            part = target.at[pl.ds(place, block.shape[0]), :]
            copies.append(pltpu.make_async_copy(block, part, sems.at[len(copies)]))
            place += block.shape[0]
    for copy in copies:
        copy.start()
    core = place_ref[0]
    tile = video.shape[0] // 2
    row = lax.broadcasted_iota(jnp.int32, (tile, PAIR), 0)
    column = lax.broadcasted_iota(jnp.int32, (tile, PAIR), 1)
    same = (row == column) & (row < PAIR // 2)

    for step in range(2):
        for copy in copies[8 + 3 * step : 11 + 3 * step]:
            copy.wait()
        rows = pl.ds(step * tile, tile)
        video_tile = video[rows, :]
        for i in range(4):
            if step == 0:
                copies[2 * i].wait()
                copies[2 * i + 1].wait()
            columns = pl.ds(i * PAIR, PAIR)
            weight = pair_weight(scale_ref, offset_ref, video_tile, text[columns, :])
            if i == 0 and step == 0:
                weight = weight - jnp.where(same, 1.0, 0.0)
            elif i == 3 and step == 1:
                weight = weight * edge_mask(core, False)
            weights[rows, columns] = weight.astype(jnp.bfloat16)


def text_sum(*pairs):
    total = None
    for weights, video in pairs:
        part = lax.dot_general(
            weights, video[...], (((0,), (0,)), ((), ())), preferred_element_type=jnp.float32
        )
        total = part if total is None else total + part
    return total


def video_sums(half, near, last_weights, far, text, last, outs):
    def dot(a, b):
        return jnp.dot(a, b[...], preferred_element_type=jnp.float32)

    tile = near.shape[0] // 2
    rows = pl.ds(half * tile, tile)
    total = dot(near[rows, :], text) + dot(last_weights[rows, :], last)
    for i, out in enumerate(outs[:3]):
        out[...] = total[i * PAIR : (i + 1) * PAIR].astype(jnp.bfloat16)
    rows = pl.ds(half * PAIR, PAIR)
    total = dot(far[rows, : 4 * PAIR], text) + dot(far[rows, 4 * PAIR :], last)
    outs[3][...] = total.astype(jnp.bfloat16)


def far_kernel(scale_ref, offset_ref, place_ref, near, text, near_video, last, *refs):
    videos, (last_weights, weights, video, below, above, *outs) = refs[:2], refs[2:]
    put(video, videos)
    core, y_hi = place_ref[0], place_ref[1]
    near_tile, rows = near_video.shape[0] // 2, PAIR // 2

    @pl.loop(0, 2)
    def _(step):
        rows = tile_rows(step, near_tile)
        weight = pair_weight(scale_ref, offset_ref, near_video[rows, :], last[...])
        last_weights[rows, :] = weight.astype(jnp.bfloat16)
        rows = tile_rows(step, PAIR)
        video_tile = video[rows, :]
        for i in range(4):
            columns = pl.ds(i * PAIR, PAIR)
            weight = pair_weight(scale_ref, offset_ref, video_tile, text[columns, :])
            if i == 3:
                weight = weight * edge_mask(core, step == 0)
            weights[rows, columns] = weight.astype(jnp.bfloat16)
        weight = pair_weight(scale_ref, offset_ref, video_tile, last[...])
        weights[rows, pl.ds(4 * PAIR, PAIR // 2)] = weight.astype(jnp.bfloat16)

    video_sums(1, near, last_weights, weights, text, last, outs)
    columns = pl.ds(3 * PAIR, PAIR)
    edges = text_sum((near[:, columns], near_video), (weights[:, columns], video))
    columns = pl.ds(4 * PAIR, rows)
    total = text_sum((last_weights[...], near_video), (weights[:, columns], video))
    below[:rows, :] = edges[:rows].astype(jnp.bfloat16)
    above[:rows, :] = edges[rows:].astype(jnp.bfloat16)
    below[rows:, :] = (total * jnp.where(y_hi == 0, 1.0, 0.0)).astype(jnp.bfloat16)
    above[rows:, :] = (total * jnp.where(y_hi == 1, 1.0, 0.0)).astype(jnp.bfloat16)


def last_kernel(near, last_weights, far, text, last, near_video, far_video, *outs):
    video_sums(0, near, last_weights, far, text, last, outs[:4])
    for i, block in enumerate(outs[4:]):
        columns = pl.ds(i * PAIR, PAIR)
        total = text_sum((near[:, columns], near_video), (far[:, columns], far_video))
        block[...] = total.astype(jnp.bfloat16)


VMEM = pl.BlockSpec(memory_space=pltpu.VMEM)
MIB = 1024 * 1024
FLOPS = 2 * N_VIDEO * N_TEXT * PAIR * PAIR * D


def low(rows, columns=D):
    return pltpu.VMEM((rows, columns), jnp.bfloat16)


def cost(flops, transcendentals=0):
    return pl.CostEstimate(flops=flops, bytes_accessed=0, transcendentals=transcendentals)


def call(kernel, name, scalars, arrays, outs, grant, flops, transcendentals=0, copies=0):
    return pl.pallas_call(
        kernel,
        out_shape=outs,
        in_specs=[SMEM] * len(scalars) + [ANY if copies else VMEM] * len(arrays),
        out_specs=[VMEM] * len(outs),
        scratch_shapes=[pltpu.SemaphoreType.DMA((copies,))] if copies else [],
        compiler_params=pltpu.CompilerParams(vmem_limit_bytes=grant * MIB),
        cost_estimate=cost(flops, transcendentals),
        name=name,
    )(*scalars, *arrays)


def local(footage_embeds, caption_embeds, score_scale, score_offset):
    blk = lax.axis_index("blk")
    core, y_hi = blk % 2, (blk // 2) % 2
    place = jnp.stack([core, y_hi]).astype(jnp.int32)
    scalars = [score_scale, score_offset, place]
    rows = footage_embeds.shape[0]
    v0, t0 = unit_low(footage_embeds, caption_embeds)

    tp, v1 = move(t0, y_hi=1), move(v0, y_lo=1)
    a1m, a1p = move(t0, z=1), move(t0, z=-1)
    v1, tp, a1m, a1p = lax.optimization_barrier((v1, tp, a1m, a1p))
    v01 = jnp.concatenate([v0, v1])
    vm, vp = move(v01, x=1), move(v01, x=-1)
    a2m, a2p = move(a1m, z=1), move(a1p, z=-1)
    b1m, b1p = move(tp, z=1), move(tp, z=-1)
    vm, vp, b1m, b1p, a2m, a2p = lax.optimization_barrier((vm, vp, b1m, b1p, a2m, a2p))
    b2 = move_by_y_hi(jnp.where(y_hi == 1, b1p, b1m))
    v2 = move_by_core(jnp.where(core == 1, vp, vm), 1)
    own = [v01, vm, vp]
    videos = own + [move(block, core=1) for block in own]
    texts = [t0, tp, a1m, b1m, a1p, b1p, a2m, a2p]

    near_rows, far_rows = 6 * PAIR, 2 * PAIR
    near, text, near_video = call(
        near_kernel,
        "near_weights",
        scalars,
        texts + videos,
        [low(near_rows, 4 * PAIR), low(4 * PAIR), low(near_rows)],
        20,
        FLOPS * 3 // 5,
        2 * near_rows * 4 * PAIR,
        len(texts + videos),
    )
    v2, b2, near = lax.optimization_barrier((v2, b2, near))
    last, far, far_video, hmm, hqq, s01, sm, sp, s2 = call(
        far_kernel,
        "far_weights_and_sums",
        scalars,
        [near, text, near_video, b2, v2, move(v2, core=1)],
        [low(near_rows, PAIR // 2), low(far_rows, 4 * PAIR + PAIR // 2), low(far_rows)]
        + [low(PAIR)] * 6,
        24,
        FLOPS * 5 // 4,
        2 * far_rows * 5 * PAIR,
    )

    r2 = move(s2, core=1)
    g01, gm, gp, g2, h01, hm, hq = call(
        last_kernel,
        "own_video_and_near_text_sums",
        [],
        [near, last, far, text, b2, near_video, far_video],
        [low(PAIR)] * 7,
        24,
        FLOPS,
    )
    hmm, hqq, r2, g01, gm, gp, g2, h01, hm, hq = lax.optimization_barrier(
        (move(hmm, z=-1), move(hqq, z=1), r2, g01, gm, gp, g2, h01, hm, hq)
    )

    up, down = move(add(hq, hqq), z=1), move(add(hm, hmm), z=-1)
    last = move(add(h01[rows:], up[rows:], down[rows:]), y_hi=1)
    text_parts = [h01, up, down, last]

    back = move_by_core(add(g2, r2), -1)
    r01, rm, rp = [move(block, core=1) for block in (s01, sm, sp)]
    none = jnp.zeros((), jnp.bfloat16)
    gm = add(gm, rm, jnp.where(core == 0, back, none))
    gp = add(gp, rp, jnp.where(core == 1, back, none))
    from_p, from_m = move(gp, x=1), move(gm, x=-1)
    last = move(add(g01[rows:], r01[rows:], from_p[rows:], from_m[rows:]), y_lo=1)
    video_parts = [g01, r01, from_p, from_m, last]

    video_grad = back_rows(score_scale, footage_embeds, video_parts)
    text_grad = back_rows(score_scale, caption_embeds, text_parts)
    return (video_grad, text_grad)


def move_by_core(block, sign):
    pairs = []
    for blk in range(4 * NZ):
        step = sign if blk % 2 == 0 else -sign
        for bulk in range(2 * NX):
            to_bulk = ((bulk // 2 + step) % NX) * 2 + bulk % 2
            pairs.append((blk * 2 * NX + bulk, blk * 2 * NX + to_bulk))
    return lax.ppermute(block, AXES, pairs)


def move_by_y_hi(block):
    pairs = []
    for blk in range(4 * NZ):
        step = 1 if (blk // 2) % 2 == 0 else -1
        to_blk = ((blk // 4 + step) % NZ) * 4 + blk % 4
        for bulk in range(2 * NX):
            pairs.append((blk * 2 * NX + bulk, to_blk * 2 * NX + bulk))
    return lax.ppermute(block, AXES, pairs)


def solution(mesh):
    assert mesh.shape["blk"] == 4 * NZ and mesh.shape["bulk"] == 2 * NX
    return jax.shard_map(
        local,
        mesh=mesh,
        in_specs=(P(AXES, None), P(AXES, None), P(), P()),
        out_specs=(P(AXES, None), P(AXES, None)),
        check_vma=False,
    )
```

```python
import functools

import jax
import jax.numpy as jnp
from jax import lax
from jax.experimental import pallas as pl
from jax.experimental.pallas import tpu as pltpu
from jax.sharding import PartitionSpec as P

EPSILON = 1e-06
NZ, NX = 8, 4
AXES = ("blk", "bulk")
SMEM = pl.BlockSpec(memory_space=pltpu.SMEM)


def move(block, x=0, z=0, y_lo=0, y_hi=0, core=0):
    pairs = []
    for blk in range(4 * NZ):
        for bulk in range(2 * NX):
            to_z = (blk // 4 + z) % NZ
            to_x = (bulk // 2 + x) % NX
            to_blk = to_z * 4 + (((blk // 2) % 2) ^ y_hi) * 2 + ((blk % 2) ^ core)
            to_bulk = to_x * 2 + ((bulk % 2) ^ y_lo)
            pairs.append((blk * 2 * NX + bulk, to_blk * 2 * NX + to_bulk))
    return lax.ppermute(block, AXES, pairs)


def add(*parts):
    total = parts[0].astype(jnp.float32)
    for part in parts[1:]:
        total = total + part.astype(jnp.float32)
    return total.astype(jnp.bfloat16)


def unit_rows(embedding):
    values = embedding.astype(jnp.float32)
    inverse = lax.rsqrt(jnp.sum(values * values, axis=1, keepdims=True) + EPSILON)
    return values * inverse, inverse


def unit_kernel(video_ref, text_ref, video_out, text_out):
    text_out[...] = unit_rows(text_ref[...])[0].astype(jnp.bfloat16)
    video_out[...] = unit_rows(video_ref[...])[0].astype(jnp.bfloat16)


def unit_low(video, text):
    shape = pltpu.VMEM(video.shape, jnp.bfloat16)
    return pl.pallas_call(unit_kernel, out_shape=(shape, shape), name="unit_low")(video, text)


def back_kernel(scale_ref, embedding_ref, *refs):
    *parts, out = refs
    rows = out.shape[0]
    total = parts[0][:rows, :].astype(jnp.float32)
    for part in parts[1:]:
        total = total + part[:rows, :].astype(jnp.float32)
    grad_unit = scale_ref[0] * total
    unit, inverse = unit_rows(embedding_ref[...])
    along = jnp.sum(unit * grad_unit, axis=1, keepdims=True)
    out[...] = (grad_unit - unit * along) * inverse


def back_rows(scale, embedding, parts):
    vmem = pl.BlockSpec(memory_space=pltpu.VMEM)
    return pl.pallas_call(
        back_kernel,
        out_shape=jax.ShapeDtypeStruct(embedding.shape, jnp.float32),
        in_specs=[SMEM] + [vmem] * (1 + len(parts)),
        out_specs=vmem,
        compiler_params=pltpu.CompilerParams(vmem_limit_bytes=5 * 1024 * 1024),
        name="back_rows",
    )(scale, embedding, *parts)


PAIR, D = 256, 768
N_TEXT, N_VIDEO = 5, 8
LOG2_E = 1.4426950408889634


def put(target, blocks):
    place = 0
    for block in blocks:
        target[pl.ds(place, block.shape[0]), :] = block[...]
        place += block.shape[0]


def pair_weight(scale_ref, offset_ref, video, text):
    products = lax.dot_general(
        video, text, (((1,), (1,)), ((), ())), preferred_element_type=jnp.float32
    )
    shifted = products * (-LOG2_E * scale_ref[0]) + -LOG2_E * offset_ref[0]
    return pl.reciprocal(1.0 + jnp.exp2(shifted), approx=True)


def edge_mask(core, own):
    half = lax.broadcasted_iota(jnp.int32, (1, PAIR), 1) < PAIR // 2
    below, above = own | (core == 1), own | (core == 0)
    return jnp.where(half, jnp.where(below, 1.0, 0.0), jnp.where(above, 1.0, 0.0))


def tile_rows(step, tile):
    return pl.ds(pl.multiple_of(step * tile, tile), tile)


def near_kernel(scale_ref, offset_ref, place_ref, *refs):
    texts, videos = refs[:8], refs[8:-3]
    weights, text, video = refs[-3:]
    put(text, texts)
    put(video, videos)
    core = place_ref[0]
    tile = video.shape[0] // 2
    row = lax.broadcasted_iota(jnp.int32, (tile, PAIR), 0)
    column = lax.broadcasted_iota(jnp.int32, (tile, PAIR), 1)
    same = (row == column) & (row < PAIR // 2)

    @pl.loop(0, 2)
    def _(step):
        rows = tile_rows(step, tile)
        video_tile = video[rows, :]
        own = step == 0
        for i in range(4):
            columns = pl.ds(i * PAIR, PAIR)
            weight = pair_weight(scale_ref, offset_ref, video_tile, text[columns, :])
            if i == 0:
                weight = weight - jnp.where(same, jnp.where(own, 1.0, 0.0), 0.0)
            elif i == 3:
                weight = weight * edge_mask(core, own)
            weights[rows, columns] = weight.astype(jnp.bfloat16)


def text_sum(*pairs):
    total = None
    for weights, video in pairs:
        part = lax.dot_general(
            weights, video[...], (((0,), (0,)), ((), ())), preferred_element_type=jnp.float32
        )
        total = part if total is None else total + part
    return total


def video_sums(half, near, last_weights, far, text, last, outs):
    def dot(a, b):
        return jnp.dot(a, b[...], preferred_element_type=jnp.float32)

    tile = near.shape[0] // 2
    rows = pl.ds(half * tile, tile)
    total = dot(near[rows, :], text) + dot(last_weights[rows, :], last)
    for i, out in enumerate(outs[:3]):
        out[...] = total[i * PAIR : (i + 1) * PAIR].astype(jnp.bfloat16)
    rows = pl.ds(half * PAIR, PAIR)
    total = dot(far[rows, : 4 * PAIR], text) + dot(far[rows, 4 * PAIR :], last)
    outs[3][...] = total.astype(jnp.bfloat16)


def far_kernel(scale_ref, offset_ref, place_ref, near, text, near_video, last, *refs):
    videos, (last_weights, weights, video, below, above, *outs) = refs[:2], refs[2:]
    put(video, videos)
    core, y_hi = place_ref[0], place_ref[1]
    near_tile, rows = near_video.shape[0] // 2, PAIR // 2

    @pl.loop(0, 2)
    def _(step):
        rows = tile_rows(step, near_tile)
        weight = pair_weight(scale_ref, offset_ref, near_video[rows, :], last[...])
        last_weights[rows, :] = weight.astype(jnp.bfloat16)
        rows = tile_rows(step, PAIR)
        video_tile = video[rows, :]
        for i in range(4):
            columns = pl.ds(i * PAIR, PAIR)
            weight = pair_weight(scale_ref, offset_ref, video_tile, text[columns, :])
            if i == 3:
                weight = weight * edge_mask(core, step == 0)
            weights[rows, columns] = weight.astype(jnp.bfloat16)
        weight = pair_weight(scale_ref, offset_ref, video_tile, last[...])
        weights[rows, pl.ds(4 * PAIR, PAIR // 2)] = weight.astype(jnp.bfloat16)

    video_sums(1, near, last_weights, weights, text, last, outs)
    columns = pl.ds(3 * PAIR, PAIR)
    edges = text_sum((near[:, columns], near_video), (weights[:, columns], video))
    columns = pl.ds(4 * PAIR, rows)
    total = text_sum((last_weights[...], near_video), (weights[:, columns], video))
    below[:rows, :] = edges[:rows].astype(jnp.bfloat16)
    above[:rows, :] = edges[rows:].astype(jnp.bfloat16)
    below[rows:, :] = (total * jnp.where(y_hi == 0, 1.0, 0.0)).astype(jnp.bfloat16)
    above[rows:, :] = (total * jnp.where(y_hi == 1, 1.0, 0.0)).astype(jnp.bfloat16)


def last_kernel(near, last_weights, far, text, last, near_video, far_video, *outs):
    video_sums(0, near, last_weights, far, text, last, outs[:4])
    for i, block in enumerate(outs[4:]):
        columns = pl.ds(i * PAIR, PAIR)
        total = text_sum((near[:, columns], near_video), (far[:, columns], far_video))
        block[...] = total.astype(jnp.bfloat16)


VMEM = pl.BlockSpec(memory_space=pltpu.VMEM)
MIB = 1024 * 1024
FLOPS = 2 * N_VIDEO * N_TEXT * PAIR * PAIR * D


def low(rows, columns=D):
    return pltpu.VMEM((rows, columns), jnp.bfloat16)


def cost(flops, transcendentals=0):
    return pl.CostEstimate(flops=flops, bytes_accessed=0, transcendentals=transcendentals)


def call(kernel, name, scalars, arrays, outs, grant, flops, transcendentals=0):
    return pl.pallas_call(
        kernel,
        out_shape=outs,
        in_specs=[SMEM] * len(scalars) + [VMEM] * len(arrays),
        out_specs=[VMEM] * len(outs),
        compiler_params=pltpu.CompilerParams(vmem_limit_bytes=grant * MIB),
        cost_estimate=cost(flops, transcendentals),
        name=name,
    )(*scalars, *arrays)


def local(footage_embeds, caption_embeds, score_scale, score_offset):
    blk = lax.axis_index("blk")
    core, y_hi = blk % 2, (blk // 2) % 2
    place = jnp.stack([core, y_hi]).astype(jnp.int32)
    scalars = [score_scale, score_offset, place]
    rows = footage_embeds.shape[0]
    v0, t0 = unit_low(footage_embeds, caption_embeds)

    tp, v1 = move(t0, y_hi=1), move(v0, y_lo=1)
    a1m, a1p = move(t0, z=1), move(t0, z=-1)
    v1, tp, a1m, a1p = lax.optimization_barrier((v1, tp, a1m, a1p))
    v01 = jnp.concatenate([v0, v1])
    vm, vp = move(v01, x=1), move(v01, x=-1)
    a2m, a2p = move(a1m, z=1), move(a1p, z=-1)
    b1m, b1p = move(tp, z=1), move(tp, z=-1)
    vm, vp, b1m, b1p, a2m, a2p = lax.optimization_barrier((vm, vp, b1m, b1p, a2m, a2p))
    b2 = move_by_y_hi(jnp.where(y_hi == 1, b1p, b1m))
    v2 = move_by_core(jnp.where(core == 1, vp, vm), 1)
    own = [v01, vm, vp]
    videos = own + [move(block, core=1) for block in own]
    texts = [t0, tp, a1m, b1m, a1p, b1p, a2m, a2p]

    near_rows, far_rows = 6 * PAIR, 2 * PAIR
    near, text, near_video = call(
        near_kernel,
        "near_weights",
        scalars,
        texts + videos,
        [low(near_rows, 4 * PAIR), low(4 * PAIR), low(near_rows)],
        8,
        FLOPS * 3 // 5,
        2 * near_rows * 4 * PAIR,
    )
    v2, b2, near = lax.optimization_barrier((v2, b2, near))
    last, far, far_video, hmm, hqq, s01, sm, sp, s2 = call(
        far_kernel,
        "far_weights_and_sums",
        scalars,
        [near, text, near_video, b2, v2, move(v2, core=1)],
        [low(near_rows, PAIR // 2), low(far_rows, 4 * PAIR + PAIR // 2), low(far_rows)]
        + [low(PAIR)] * 6,
        11,
        FLOPS * 5 // 4,
        2 * far_rows * 5 * PAIR,
    )

    r2 = move(s2, core=1)
    g01, gm, gp, g2, h01, hm, hq = call(
        last_kernel,
        "own_video_and_near_text_sums",
        [],
        [near, last, far, text, b2, near_video, far_video],
        [low(PAIR)] * 7,
        11,
        FLOPS,
    )
    hmm, hqq, r2, g01, gm, gp, g2, h01, hm, hq = lax.optimization_barrier(
        (move(hmm, z=-1), move(hqq, z=1), r2, g01, gm, gp, g2, h01, hm, hq)
    )

    up, down = move(add(hq, hqq), z=1), move(add(hm, hmm), z=-1)
    last = move(add(h01[rows:], up[rows:], down[rows:]), y_hi=1)
    text_parts = [h01, up, down, last]

    back = move_by_core(add(g2, r2), -1)
    r01, rm, rp = [move(block, core=1) for block in (s01, sm, sp)]
    none = jnp.zeros((), jnp.bfloat16)
    gm = add(gm, rm, jnp.where(core == 0, back, none))
    gp = add(gp, rp, jnp.where(core == 1, back, none))
    from_p, from_m = move(gp, x=1), move(gm, x=-1)
    last = move(add(g01[rows:], r01[rows:], from_p[rows:], from_m[rows:]), y_lo=1)
    video_parts = [g01, r01, from_p, from_m, last]

    video_grad = back_rows(score_scale, footage_embeds, video_parts)
    text_grad = back_rows(score_scale, caption_embeds, text_parts)
    return (video_grad, text_grad)


def move_by_core(block, sign):
    pairs = []
    for blk in range(4 * NZ):
        step = sign if blk % 2 == 0 else -sign
        for bulk in range(2 * NX):
            to_bulk = ((bulk // 2 + step) % NX) * 2 + bulk % 2
            pairs.append((blk * 2 * NX + bulk, blk * 2 * NX + to_bulk))
    return lax.ppermute(block, AXES, pairs)


def move_by_y_hi(block):
    pairs = []
    for blk in range(4 * NZ):
        step = 1 if (blk // 2) % 2 == 0 else -1
        to_blk = ((blk // 4 + step) % NZ) * 4 + blk % 4
        for bulk in range(2 * NX):
            pairs.append((blk * 2 * NX + bulk, to_blk * 2 * NX + bulk))
    return lax.ppermute(block, AXES, pairs)


def solution(mesh):
    assert mesh.shape["blk"] == 4 * NZ and mesh.shape["bulk"] == 2 * NX
    return jax.shard_map(
        local,
        mesh=mesh,
        in_specs=(P(AXES, None), P(AXES, None), P(), P()),
        out_specs=(P(AXES, None), P(AXES, None)),
        check_vma=False,
    )
```

```python
import functools

import jax
import jax.numpy as jnp
from jax import lax
from jax.experimental import pallas as pl
from jax.experimental.pallas import tpu as pltpu
from jax.sharding import PartitionSpec as P

EPSILON = 1e-06
NZ, NX = 8, 4
AXES = ("blk", "bulk")
SMEM = pl.BlockSpec(memory_space=pltpu.SMEM)


def move(block, x=0, z=0, y_lo=0, y_hi=0, core=0):
    pairs = []
    for blk in range(4 * NZ):
        for bulk in range(2 * NX):
            to_z = (blk // 4 + z) % NZ
            to_x = (bulk // 2 + x) % NX
            to_blk = to_z * 4 + (((blk // 2) % 2) ^ y_hi) * 2 + ((blk % 2) ^ core)
            to_bulk = to_x * 2 + ((bulk % 2) ^ y_lo)
            pairs.append((blk * 2 * NX + bulk, to_blk * 2 * NX + to_bulk))
    return lax.ppermute(block, AXES, pairs)


def add(*parts):
    total = parts[0].astype(jnp.float32)
    for part in parts[1:]:
        total = total + part.astype(jnp.float32)
    return total.astype(jnp.bfloat16)


def unit_rows(embedding):
    values = embedding.astype(jnp.float32)
    inverse = lax.rsqrt(jnp.sum(values * values, axis=1, keepdims=True) + EPSILON)
    return values * inverse, inverse


def unit_kernel(video_ref, text_ref, video_out, text_out):
    text_out[...] = unit_rows(text_ref[...])[0].astype(jnp.bfloat16)
    video_out[...] = unit_rows(video_ref[...])[0].astype(jnp.bfloat16)


def unit_low(video, text):
    shape = pltpu.VMEM(video.shape, jnp.bfloat16)
    return pl.pallas_call(unit_kernel, out_shape=(shape, shape), name="unit_low")(video, text)


def back_kernel(scale_ref, embedding_ref, *refs):
    *parts, out = refs
    rows = out.shape[0]
    total = parts[0][:rows, :].astype(jnp.float32)
    for part in parts[1:]:
        total = total + part[:rows, :].astype(jnp.float32)
    grad_unit = scale_ref[0] * total
    unit, inverse = unit_rows(embedding_ref[...])
    along = jnp.sum(unit * grad_unit, axis=1, keepdims=True)
    out[...] = (grad_unit - unit * along) * inverse


def back_rows(scale, embedding, parts):
    vmem = pl.BlockSpec(memory_space=pltpu.VMEM)
    return pl.pallas_call(
        back_kernel,
        out_shape=jax.ShapeDtypeStruct(embedding.shape, jnp.float32),
        in_specs=[SMEM] + [vmem] * (1 + len(parts)),
        out_specs=vmem,
        compiler_params=pltpu.CompilerParams(vmem_limit_bytes=5 * 1024 * 1024),
        name="back_rows",
    )(scale, embedding, *parts)


PAIR, D = 256, 768
N_TEXT, N_VIDEO = 5, 8
LOG2_E = 1.4426950408889634


def put(target, blocks):
    place = 0
    for block in blocks:
        target[pl.ds(place, block.shape[0]), :] = block[...]
        place += block.shape[0]


def pair_weight(scale_ref, offset_ref, video, text):
    products = lax.dot_general(
        video, text, (((1,), (1,)), ((), ())), preferred_element_type=jnp.float32
    )
    shifted = products * (-LOG2_E * scale_ref[0]) + -LOG2_E * offset_ref[0]
    return pl.reciprocal(1.0 + jnp.exp2(shifted), approx=True)


def edge_mask(core, own):
    half = lax.broadcasted_iota(jnp.int32, (1, PAIR), 1) < PAIR // 2
    below, above = own | (core == 1), own | (core == 0)
    return jnp.where(half, jnp.where(below, 1.0, 0.0), jnp.where(above, 1.0, 0.0))


def tile_rows(step, tile):
    return pl.ds(pl.multiple_of(step * tile, tile), tile)


def near_kernel(scale_ref, offset_ref, place_ref, *refs):
    texts, videos = refs[:8], refs[8:-3]
    weights, text, video = refs[-3:]
    put(text, texts)
    put(video, videos)
    core = place_ref[0]
    tile = video.shape[0] // 2
    row = lax.broadcasted_iota(jnp.int32, (tile, PAIR), 0)
    column = lax.broadcasted_iota(jnp.int32, (tile, PAIR), 1)
    same = (row == column) & (row < PAIR // 2)

    @pl.loop(0, 2)
    def _(step):
        rows = tile_rows(step, tile)
        video_tile = video[rows, :]
        own = step == 0
        for i in range(4):
            columns = pl.ds(i * PAIR, PAIR)
            weight = pair_weight(scale_ref, offset_ref, video_tile, text[columns, :])
            if i == 0:
                weight = weight - jnp.where(same, jnp.where(own, 1.0, 0.0), 0.0)
            elif i == 3:
                weight = weight * edge_mask(core, own)
            weights[rows, columns] = weight.astype(jnp.bfloat16)


def text_sum(*pairs):
    total = None
    for weights, video in pairs:
        part = lax.dot_general(
            weights, video[...], (((0,), (0,)), ((), ())), preferred_element_type=jnp.float32
        )
        total = part if total is None else total + part
    return total


def video_sums(half, near, last_weights, far, text, last, outs):
    def dot(a, b):
        return jnp.dot(a, b[...], preferred_element_type=jnp.float32)

    tile = near.shape[0] // 2
    rows = pl.ds(half * tile, tile)
    total = dot(near[rows, :], text) + dot(last_weights[rows, :], last)
    for i, out in enumerate(outs[:3]):
        out[...] = total[i * PAIR : (i + 1) * PAIR].astype(jnp.bfloat16)
    rows = pl.ds(half * PAIR, PAIR)
    total = dot(far[rows, : 4 * PAIR], text) + dot(far[rows, 4 * PAIR :], last)
    outs[3][...] = total.astype(jnp.bfloat16)


def far_kernel(scale_ref, offset_ref, place_ref, near, text, near_video, last, *refs):
    videos, (below, above, *outs), scratch = refs[:2], refs[2:-3], refs[-3:]
    last_weights, weights, video = scratch
    put(video, videos)
    core, y_hi = place_ref[0], place_ref[1]
    near_tile, rows = near_video.shape[0] // 2, PAIR // 2

    @pl.loop(0, 2)
    def _(step):
        rows = tile_rows(step, near_tile)
        weight = pair_weight(scale_ref, offset_ref, near_video[rows, :], last[...])
        last_weights[rows, :] = weight.astype(jnp.bfloat16)
        rows = tile_rows(step, PAIR)
        video_tile = video[rows, :]
        for i in range(4):
            columns = pl.ds(i * PAIR, PAIR)
            weight = pair_weight(scale_ref, offset_ref, video_tile, text[columns, :])
            if i == 3:
                weight = weight * edge_mask(core, step == 0)
            weights[rows, columns] = weight.astype(jnp.bfloat16)
        weight = pair_weight(scale_ref, offset_ref, video_tile, last[...])
        weights[rows, pl.ds(4 * PAIR, PAIR // 2)] = weight.astype(jnp.bfloat16)

    video_sums(1, near, last_weights, weights, text, last, outs[:4])
    video_sums(0, near, last_weights, weights, text, last, outs[4:8])
    for i, block in enumerate(outs[8:]):
        columns = pl.ds(i * PAIR, PAIR)
        total = text_sum((near[:, columns], near_video), (weights[:, columns], video))
        block[...] = total.astype(jnp.bfloat16)
    columns = pl.ds(3 * PAIR, PAIR)
    edges = text_sum((near[:, columns], near_video), (weights[:, columns], video))
    columns = pl.ds(4 * PAIR, rows)
    total = text_sum((last_weights[...], near_video), (weights[:, columns], video))
    below[:rows, :] = edges[:rows].astype(jnp.bfloat16)
    above[:rows, :] = edges[rows:].astype(jnp.bfloat16)
    below[rows:, :] = (total * jnp.where(y_hi == 0, 1.0, 0.0)).astype(jnp.bfloat16)
    above[rows:, :] = (total * jnp.where(y_hi == 1, 1.0, 0.0)).astype(jnp.bfloat16)


VMEM = pl.BlockSpec(memory_space=pltpu.VMEM)
MIB = 1024 * 1024
FLOPS = 2 * N_VIDEO * N_TEXT * PAIR * PAIR * D


def low(rows, columns=D):
    return pltpu.VMEM((rows, columns), jnp.bfloat16)


def cost(flops, transcendentals=0):
    return pl.CostEstimate(flops=flops, bytes_accessed=0, transcendentals=transcendentals)


def call(kernel, name, scalars, arrays, outs, grant, flops, transcendentals, scratch=()):
    return pl.pallas_call(
        kernel,
        out_shape=outs,
        in_specs=[SMEM] * len(scalars) + [VMEM] * len(arrays),
        out_specs=[VMEM] * len(outs),
        scratch_shapes=scratch,
        compiler_params=pltpu.CompilerParams(vmem_limit_bytes=grant * MIB),
        cost_estimate=cost(flops, transcendentals),
        name=name,
    )(*scalars, *arrays)


def local(footage_embeds, caption_embeds, score_scale, score_offset):
    blk = lax.axis_index("blk")
    core, y_hi = blk % 2, (blk // 2) % 2
    place = jnp.stack([core, y_hi]).astype(jnp.int32)
    scalars = [score_scale, score_offset, place]
    rows = footage_embeds.shape[0]
    v0, t0 = unit_low(footage_embeds, caption_embeds)

    tp, v1 = move(t0, y_hi=1), move(v0, y_lo=1)
    a1m, a1p = move(t0, z=1), move(t0, z=-1)
    v1, tp, a1m, a1p = lax.optimization_barrier((v1, tp, a1m, a1p))
    v01 = jnp.concatenate([v0, v1])
    vm, vp = move(v01, x=1), move(v01, x=-1)
    a2m, a2p = move(a1m, z=1), move(a1p, z=-1)
    b1m, b1p = move(tp, z=1), move(tp, z=-1)
    vm, vp, b1m, b1p, a2m, a2p = lax.optimization_barrier((vm, vp, b1m, b1p, a2m, a2p))
    b2 = move_by_y_hi(jnp.where(y_hi == 1, b1p, b1m))
    v2 = move_by_core(jnp.where(core == 1, vp, vm), 1)
    own = [v01, vm, vp]
    videos = own + [move(block, core=1) for block in own]
    texts = [t0, tp, a1m, b1m, a1p, b1p, a2m, a2p]

    near_rows, far_rows = 6 * PAIR, 2 * PAIR
    near, text, near_video = call(
        near_kernel,
        "near_weights",
        scalars,
        texts + videos,
        [low(near_rows, 4 * PAIR), low(4 * PAIR), low(near_rows)],
        8,
        FLOPS * 3 // 5,
        2 * near_rows * 4 * PAIR,
    )
    v2, b2, near = lax.optimization_barrier((v2, b2, near))
    hmm, hqq, s01, sm, sp, s2, g01, gm, gp, g2, h01, hm, hq = call(
        far_kernel,
        "far_weights_and_sums",
        scalars,
        [near, text, near_video, b2, v2, move(v2, core=1)],
        [low(PAIR)] * 13,
        14,
        FLOPS * 9 // 4,
        2 * far_rows * 5 * PAIR,
        [low(near_rows, PAIR // 2), low(far_rows, 4 * PAIR + PAIR // 2), low(far_rows)],
    )

    back = move_by_core(add(g2, move(s2, core=1)), -1)
    hmm, hqq, back = lax.optimization_barrier((move(hmm, z=-1), move(hqq, z=1), back))
    up, down = move(add(hq, hqq), z=1), move(add(hm, hmm), z=-1)
    last = move(add(h01[rows:], up[rows:], down[rows:]), y_hi=1)
    text_parts = [h01, up, down, last]

    r01, rm, rp = [move(block, core=1) for block in (s01, sm, sp)]
    none = jnp.zeros((), jnp.bfloat16)
    gm = add(gm, rm, jnp.where(core == 0, back, none))
    gp = add(gp, rp, jnp.where(core == 1, back, none))
    from_p, from_m = move(gp, x=1), move(gm, x=-1)
    last = move(add(g01[rows:], r01[rows:], from_p[rows:], from_m[rows:]), y_lo=1)
    video_parts = [g01, r01, from_p, from_m, last]

    video_grad = back_rows(score_scale, footage_embeds, video_parts)
    text_grad = back_rows(score_scale, caption_embeds, text_parts)
    return (video_grad, text_grad)


def move_by_core(block, sign):
    pairs = []
    for blk in range(4 * NZ):
        step = sign if blk % 2 == 0 else -sign
        for bulk in range(2 * NX):
            to_bulk = ((bulk // 2 + step) % NX) * 2 + bulk % 2
            pairs.append((blk * 2 * NX + bulk, blk * 2 * NX + to_bulk))
    return lax.ppermute(block, AXES, pairs)


def move_by_y_hi(block):
    pairs = []
    for blk in range(4 * NZ):
        step = 1 if (blk // 2) % 2 == 0 else -1
        to_blk = ((blk // 4 + step) % NZ) * 4 + blk % 4
        for bulk in range(2 * NX):
            pairs.append((blk * 2 * NX + bulk, to_blk * 2 * NX + bulk))
    return lax.ppermute(block, AXES, pairs)


def solution(mesh):
    assert mesh.shape["blk"] == 4 * NZ and mesh.shape["bulk"] == 2 * NX
    return jax.shard_map(
        local,
        mesh=mesh,
        in_specs=(P(AXES, None), P(AXES, None), P(), P()),
        out_specs=(P(AXES, None), P(AXES, None)),
        check_vma=False,
    )
```

```python
import functools

import jax
import jax.numpy as jnp
from jax import lax
from jax.experimental import pallas as pl
from jax.experimental.pallas import tpu as pltpu
from jax.sharding import PartitionSpec as P

EPSILON = 1e-06
NZ, NX = 8, 4
AXES = ("blk", "bulk")
SMEM = pl.BlockSpec(memory_space=pltpu.SMEM)


def move(block, x=0, z=0, y_lo=0, y_hi=0, core=0):
    pairs = []
    for blk in range(4 * NZ):
        for bulk in range(2 * NX):
            to_z = (blk // 4 + z) % NZ
            to_x = (bulk // 2 + x) % NX
            to_blk = to_z * 4 + (((blk // 2) % 2) ^ y_hi) * 2 + ((blk % 2) ^ core)
            to_bulk = to_x * 2 + ((bulk % 2) ^ y_lo)
            pairs.append((blk * 2 * NX + bulk, to_blk * 2 * NX + to_bulk))
    return lax.ppermute(block, AXES, pairs)


def add(*parts):
    total = parts[0].astype(jnp.float32)
    for part in parts[1:]:
        total = total + part.astype(jnp.float32)
    return total.astype(jnp.bfloat16)


def unit_rows(embedding):
    values = embedding.astype(jnp.float32)
    inverse = lax.rsqrt(jnp.sum(values * values, axis=1, keepdims=True) + EPSILON)
    return values * inverse, inverse


def unit_kernel(video_ref, text_ref, video_out, text_out):
    text_out[...] = unit_rows(text_ref[...])[0].astype(jnp.bfloat16)
    video_out[...] = unit_rows(video_ref[...])[0].astype(jnp.bfloat16)


def unit_low(video, text):
    shape = pltpu.VMEM(video.shape, jnp.bfloat16)
    return pl.pallas_call(unit_kernel, out_shape=(shape, shape), name="unit_low")(video, text)


def back_kernel(scale_ref, embedding_ref, *refs):
    *parts, out = refs
    rows = out.shape[0]
    total = parts[0][:rows, :].astype(jnp.float32)
    for part in parts[1:]:
        total = total + part[:rows, :].astype(jnp.float32)
    grad_unit = scale_ref[0] * total
    unit, inverse = unit_rows(embedding_ref[...])
    along = jnp.sum(unit * grad_unit, axis=1, keepdims=True)
    out[...] = (grad_unit - unit * along) * inverse


def back_rows(scale, embedding, parts):
    vmem = pl.BlockSpec(memory_space=pltpu.VMEM)
    return pl.pallas_call(
        back_kernel,
        out_shape=jax.ShapeDtypeStruct(embedding.shape, jnp.float32),
        in_specs=[SMEM] + [vmem] * (1 + len(parts)),
        out_specs=vmem,
        compiler_params=pltpu.CompilerParams(vmem_limit_bytes=5 * 1024 * 1024),
        name="back_rows",
    )(scale, embedding, *parts)


PAIR, D = 256, 768
N_TEXT, N_VIDEO = 5, 8
LOG2_E = 1.4426950408889634


def put(target, blocks):
    place = 0
    for block in blocks:
        target[pl.ds(place, block.shape[0]), :] = block[...]
        place += block.shape[0]


def pair_weight(scale_ref, offset_ref, video, text):
    products = lax.dot_general(
        video, text, (((1,), (1,)), ((), ())), preferred_element_type=jnp.float32
    )
    shifted = products * (-LOG2_E * scale_ref[0]) + -LOG2_E * offset_ref[0]
    return pl.reciprocal(1.0 + jnp.exp2(shifted), approx=True)


def edge_mask(core, own):
    half = lax.broadcasted_iota(jnp.int32, (1, PAIR), 1) < PAIR // 2
    below, above = own | (core == 1), own | (core == 0)
    return jnp.where(half, jnp.where(below, 1.0, 0.0), jnp.where(above, 1.0, 0.0))


def tile_rows(step, tile):
    return pl.ds(pl.multiple_of(step * tile, tile), tile)


def near_kernel(scale_ref, offset_ref, place_ref, *refs):
    texts, videos = refs[:8], refs[8:-3]
    weights, text, video = refs[-3:]
    put(text, texts)
    put(video, videos)
    core = place_ref[0]
    tile = video.shape[0] // 2
    row = lax.broadcasted_iota(jnp.int32, (tile, PAIR), 0)
    column = lax.broadcasted_iota(jnp.int32, (tile, PAIR), 1)
    same = (row == column) & (row < PAIR // 2)

    @pl.loop(0, 2)
    def _(step):
        rows = tile_rows(step, tile)
        video_tile = video[rows, :]
        own = step == 0
        for i in range(4):
            columns = pl.ds(i * PAIR, PAIR)
            weight = pair_weight(scale_ref, offset_ref, video_tile, text[columns, :])
            if i == 0:
                weight = weight - jnp.where(same, jnp.where(own, 1.0, 0.0), 0.0)
            elif i == 3:
                weight = weight * edge_mask(core, own)
            weights[rows, columns] = weight.astype(jnp.bfloat16)


def text_sum(*pairs):
    total = None
    for weights, video in pairs:
        part = lax.dot_general(
            weights, video[...], (((0,), (0,)), ((), ())), preferred_element_type=jnp.float32
        )
        total = part if total is None else total + part
    return total


def video_sums(half, near, last_weights, far, text, last, outs):
    def dot(a, b):
        return jnp.dot(a, b[...], preferred_element_type=jnp.float32)

    for i, out in enumerate(outs[:3]):
        rows = pl.ds(half * (near.shape[0] // 2) + i * PAIR, PAIR)
        total = dot(near[rows, :], text) + dot(last_weights[rows, :], last)
        out[...] = total.astype(jnp.bfloat16)
    rows = pl.ds(half * PAIR, PAIR)
    total = dot(far[rows, : 4 * PAIR], text) + dot(far[rows, 4 * PAIR :], last)
    outs[3][...] = total.astype(jnp.bfloat16)


def far_kernel(scale_ref, offset_ref, place_ref, near, text, near_video, last, *refs):
    videos, (last_weights, weights, video, below, above, *outs) = refs[:2], refs[2:]
    put(video, videos)
    core, y_hi = place_ref[0], place_ref[1]
    near_tile, rows = near_video.shape[0] // 2, PAIR // 2

    @pl.loop(0, 2)
    def _(step):
        rows = tile_rows(step, near_tile)
        weight = pair_weight(scale_ref, offset_ref, near_video[rows, :], last[...])
        last_weights[rows, :] = weight.astype(jnp.bfloat16)
        rows = tile_rows(step, PAIR)
        video_tile = video[rows, :]
        for i in range(4):
            columns = pl.ds(i * PAIR, PAIR)
            weight = pair_weight(scale_ref, offset_ref, video_tile, text[columns, :])
            if i == 3:
                weight = weight * edge_mask(core, step == 0)
            weights[rows, columns] = weight.astype(jnp.bfloat16)
        weight = pair_weight(scale_ref, offset_ref, video_tile, last[...])
        weights[rows, pl.ds(4 * PAIR, PAIR // 2)] = weight.astype(jnp.bfloat16)

    video_sums(1, near, last_weights, weights, text, last, outs)
    columns = pl.ds(3 * PAIR, PAIR)
    edges = text_sum((near[:, columns], near_video), (weights[:, columns], video))
    columns = pl.ds(4 * PAIR, rows)
    total = text_sum((last_weights[...], near_video), (weights[:, columns], video))
    below[:rows, :] = edges[:rows].astype(jnp.bfloat16)
    above[:rows, :] = edges[rows:].astype(jnp.bfloat16)
    below[rows:, :] = (total * jnp.where(y_hi == 0, 1.0, 0.0)).astype(jnp.bfloat16)
    above[rows:, :] = (total * jnp.where(y_hi == 1, 1.0, 0.0)).astype(jnp.bfloat16)


def last_kernel(near, last_weights, far, text, last, near_video, far_video, *outs):
    video_sums(0, near, last_weights, far, text, last, outs[:4])
    for i, block in enumerate(outs[4:]):
        columns = pl.ds(i * PAIR, PAIR)
        total = text_sum((near[:, columns], near_video), (far[:, columns], far_video))
        block[...] = total.astype(jnp.bfloat16)


VMEM = pl.BlockSpec(memory_space=pltpu.VMEM)
MIB = 1024 * 1024
FLOPS = 2 * N_VIDEO * N_TEXT * PAIR * PAIR * D


def low(rows, columns=D):
    return pltpu.VMEM((rows, columns), jnp.bfloat16)


def cost(flops, transcendentals=0):
    return pl.CostEstimate(flops=flops, bytes_accessed=0, transcendentals=transcendentals)


def call(kernel, name, scalars, arrays, outs, grant, flops, transcendentals=0):
    return pl.pallas_call(
        kernel,
        out_shape=outs,
        in_specs=[SMEM] * len(scalars) + [VMEM] * len(arrays),
        out_specs=[VMEM] * len(outs),
        compiler_params=pltpu.CompilerParams(vmem_limit_bytes=grant * MIB),
        cost_estimate=cost(flops, transcendentals),
        name=name,
    )(*scalars, *arrays)


def local(footage_embeds, caption_embeds, score_scale, score_offset):
    blk = lax.axis_index("blk")
    core, y_hi = blk % 2, (blk // 2) % 2
    place = jnp.stack([core, y_hi]).astype(jnp.int32)
    scalars = [score_scale, score_offset, place]
    rows = footage_embeds.shape[0]
    v0, t0 = unit_low(footage_embeds, caption_embeds)

    tp, v1 = move(t0, y_hi=1), move(v0, y_lo=1)
    a1m, a1p = move(t0, z=1), move(t0, z=-1)
    v1, tp, a1m, a1p = lax.optimization_barrier((v1, tp, a1m, a1p))
    v01 = jnp.concatenate([v0, v1])
    vm, vp = move(v01, x=1), move(v01, x=-1)
    a2m, a2p = move(a1m, z=1), move(a1p, z=-1)
    b1m, b1p = move(tp, z=1), move(tp, z=-1)
    vm, vp, b1m, b1p, a2m, a2p = lax.optimization_barrier((vm, vp, b1m, b1p, a2m, a2p))
    b2 = move_by_y_hi(jnp.where(y_hi == 1, b1p, b1m))
    v2 = move_by_core(jnp.where(core == 1, vp, vm), 1)
    own = [v01, vm, vp]
    videos = own + [move(block, core=1) for block in own]
    texts = [t0, tp, a1m, b1m, a1p, b1p, a2m, a2p]

    near_rows, far_rows = 6 * PAIR, 2 * PAIR
    near, text, near_video = call(
        near_kernel,
        "near_weights",
        scalars,
        texts + videos,
        [low(near_rows, 4 * PAIR), low(4 * PAIR), low(near_rows)],
        4,
        FLOPS * 3 // 5,
        2 * near_rows * 4 * PAIR,
    )
    v2, b2, near = lax.optimization_barrier((v2, b2, near))
    last, far, far_video, hmm, hqq, s01, sm, sp, s2 = call(
        far_kernel,
        "far_weights_and_sums",
        scalars,
        [near, text, near_video, b2, v2, move(v2, core=1)],
        [low(near_rows, PAIR // 2), low(far_rows, 4 * PAIR + PAIR // 2), low(far_rows)]
        + [low(PAIR)] * 6,
        4,
        FLOPS * 5 // 4,
        2 * far_rows * 5 * PAIR,
    )

    r2 = move(s2, core=1)
    g01, gm, gp, g2, h01, hm, hq = call(
        last_kernel,
        "own_video_and_near_text_sums",
        [],
        [near, last, far, text, b2, near_video, far_video],
        [low(PAIR)] * 7,
        4,
        FLOPS,
    )
    back = move_by_core(add(g2, r2), -1)
    hmm, hqq, back, g01, gm, gp, h01, hm, hq = lax.optimization_barrier(
        (move(hmm, z=-1), move(hqq, z=1), back, g01, gm, gp, h01, hm, hq)
    )

    up, down = move(add(hq, hqq), z=1), move(add(hm, hmm), z=-1)
    last = move(add(h01[rows:], up[rows:], down[rows:]), y_hi=1)
    text_parts = [h01, up, down, last]

    r01, rm, rp = [move(block, core=1) for block in (s01, sm, sp)]
    none = jnp.zeros((), jnp.bfloat16)
    gm = add(gm, rm, jnp.where(core == 0, back, none))
    gp = add(gp, rp, jnp.where(core == 1, back, none))
    from_p, from_m = move(gp, x=1), move(gm, x=-1)
    last = move(add(g01[rows:], r01[rows:], from_p[rows:], from_m[rows:]), y_lo=1)
    video_parts = [g01, r01, from_p, from_m, last]

    video_grad = back_rows(score_scale, footage_embeds, video_parts)
    text_grad = back_rows(score_scale, caption_embeds, text_parts)
    return (video_grad, text_grad)


def move_by_core(block, sign):
    pairs = []
    for blk in range(4 * NZ):
        step = sign if blk % 2 == 0 else -sign
        for bulk in range(2 * NX):
            to_bulk = ((bulk // 2 + step) % NX) * 2 + bulk % 2
            pairs.append((blk * 2 * NX + bulk, blk * 2 * NX + to_bulk))
    return lax.ppermute(block, AXES, pairs)


def move_by_y_hi(block):
    pairs = []
    for blk in range(4 * NZ):
        step = 1 if (blk // 2) % 2 == 0 else -1
        to_blk = ((blk // 4 + step) % NZ) * 4 + blk % 4
        for bulk in range(2 * NX):
            pairs.append((blk * 2 * NX + bulk, to_blk * 2 * NX + bulk))
    return lax.ppermute(block, AXES, pairs)


def solution(mesh):
    assert mesh.shape["blk"] == 4 * NZ and mesh.shape["bulk"] == 2 * NX
    return jax.shard_map(
        local,
        mesh=mesh,
        in_specs=(P(AXES, None), P(AXES, None), P(), P()),
        out_specs=(P(AXES, None), P(AXES, None)),
        check_vma=False,
    )
```

```python
import functools

import jax
import jax.numpy as jnp
from jax import lax
from jax.experimental import pallas as pl
from jax.experimental.pallas import tpu as pltpu
from jax.sharding import PartitionSpec as P

EPSILON = 1e-06
NZ, NX = 8, 4
AXES = ("blk", "bulk")
SMEM = pl.BlockSpec(memory_space=pltpu.SMEM)


def move(block, x=0, z=0, y_lo=0, y_hi=0, core=0):
    pairs = []
    for blk in range(4 * NZ):
        for bulk in range(2 * NX):
            to_z = (blk // 4 + z) % NZ
            to_x = (bulk // 2 + x) % NX
            to_blk = to_z * 4 + (((blk // 2) % 2) ^ y_hi) * 2 + ((blk % 2) ^ core)
            to_bulk = to_x * 2 + ((bulk % 2) ^ y_lo)
            pairs.append((blk * 2 * NX + bulk, to_blk * 2 * NX + to_bulk))
    return lax.ppermute(block, AXES, pairs)


def add(*parts):
    total = parts[0].astype(jnp.float32)
    for part in parts[1:]:
        total = total + part.astype(jnp.float32)
    return total.astype(jnp.bfloat16)


def unit_rows(embedding):
    values = embedding.astype(jnp.float32)
    inverse = lax.rsqrt(jnp.sum(values * values, axis=1, keepdims=True) + EPSILON)
    return values * inverse, inverse


def unit_kernel(video_ref, text_ref, video_out, text_out):
    text_out[...] = unit_rows(text_ref[...])[0].astype(jnp.bfloat16)
    video_out[...] = unit_rows(video_ref[...])[0].astype(jnp.bfloat16)


def unit_low(video, text):
    shape = pltpu.VMEM(video.shape, jnp.bfloat16)
    return pl.pallas_call(unit_kernel, out_shape=(shape, shape), name="unit_low")(video, text)


def back_kernel(scale_ref, embedding_ref, *refs):
    *parts, out = refs
    rows = out.shape[0]
    total = parts[0][:rows, :].astype(jnp.float32)
    for part in parts[1:]:
        total = total + part[:rows, :].astype(jnp.float32)
    grad_unit = scale_ref[0] * total
    unit, inverse = unit_rows(embedding_ref[...])
    along = jnp.sum(unit * grad_unit, axis=1, keepdims=True)
    out[...] = (grad_unit - unit * along) * inverse


def back_rows(scale, embedding, parts):
    vmem = pl.BlockSpec(memory_space=pltpu.VMEM)
    return pl.pallas_call(
        back_kernel,
        out_shape=jax.ShapeDtypeStruct(embedding.shape, jnp.float32),
        in_specs=[SMEM] + [vmem] * (1 + len(parts)),
        out_specs=vmem,
        compiler_params=pltpu.CompilerParams(vmem_limit_bytes=5 * 1024 * 1024),
        name="back_rows",
    )(scale, embedding, *parts)


PAIR, D = 256, 768
N_TEXT, N_VIDEO = 5, 8
LOG2_E = 1.4426950408889634


def put(target, blocks):
    place = 0
    for block in blocks:
        target[pl.ds(place, block.shape[0]), :] = block[...]
        place += block.shape[0]


def pair_weight(scale_ref, offset_ref, video, text):
    products = lax.dot_general(
        video, text, (((1,), (1,)), ((), ())), preferred_element_type=jnp.float32
    )
    shifted = products * (-LOG2_E * scale_ref[0]) + -LOG2_E * offset_ref[0]
    return pl.reciprocal(1.0 + jnp.exp2(shifted), approx=True)


def edge_mask(core, own):
    half = lax.broadcasted_iota(jnp.int32, (1, PAIR), 1) < PAIR // 2
    below, above = own | (core == 1), own | (core == 0)
    return jnp.where(half, jnp.where(below, 1.0, 0.0), jnp.where(above, 1.0, 0.0))


def tile_rows(step, tile):
    return pl.ds(pl.multiple_of(step * tile, tile), tile)


def near_kernel(scale_ref, offset_ref, place_ref, *refs):
    texts, videos = refs[:8], refs[8:-3]
    weights, text, video = refs[-3:]
    put(text, texts)
    put(video, videos)
    core = place_ref[0]
    tile = video.shape[0] // 2
    row = lax.broadcasted_iota(jnp.int32, (tile, PAIR), 0)
    column = lax.broadcasted_iota(jnp.int32, (tile, PAIR), 1)
    same = (row == column) & (row < PAIR // 2)

    @pl.loop(0, 2)
    def _(step):
        rows = tile_rows(step, tile)
        video_tile = video[rows, :]
        own = step == 0
        for i in range(4):
            columns = pl.ds(i * PAIR, PAIR)
            weight = pair_weight(scale_ref, offset_ref, video_tile, text[columns, :])
            if i == 0:
                weight = weight - jnp.where(same, jnp.where(own, 1.0, 0.0), 0.0)
            elif i == 3:
                weight = weight * edge_mask(core, own)
            weights[rows, columns] = weight.astype(jnp.bfloat16)


def text_sum(*pairs):
    total = None
    for weights, video in pairs:
        part = lax.dot_general(
            weights, video[...], (((0,), (0,)), ((), ())), preferred_element_type=jnp.float32
        )
        total = part if total is None else total + part
    return total


def video_sums(half, near, last_weights, far, text, last, outs):
    def dot(a, b):
        return jnp.dot(a, b[...], preferred_element_type=jnp.float32)

    for i, out in enumerate(outs[:3]):
        rows = pl.ds(half * (near.shape[0] // 2) + i * PAIR, PAIR)
        total = dot(near[rows, :], text) + dot(last_weights[rows, :], last)
        out[...] = total.astype(jnp.bfloat16)
    rows = pl.ds(half * PAIR, PAIR)
    total = dot(far[rows, : 4 * PAIR], text) + dot(far[rows, 4 * PAIR :], last)
    outs[3][...] = total.astype(jnp.bfloat16)


def far_kernel(scale_ref, offset_ref, place_ref, near, text, near_video, last, *refs):
    videos, (last_weights, weights, video, below, above, *outs) = refs[:2], refs[2:]
    put(video, videos)
    core, y_hi = place_ref[0], place_ref[1]
    near_tile, rows = near_video.shape[0] // 2, PAIR // 2

    @pl.loop(0, 2)
    def _(step):
        rows = tile_rows(step, near_tile)
        weight = pair_weight(scale_ref, offset_ref, near_video[rows, :], last[...])
        last_weights[rows, :] = weight.astype(jnp.bfloat16)
        rows = tile_rows(step, PAIR)
        video_tile = video[rows, :]
        for i in range(4):
            columns = pl.ds(i * PAIR, PAIR)
            weight = pair_weight(scale_ref, offset_ref, video_tile, text[columns, :])
            if i == 3:
                weight = weight * edge_mask(core, step == 0)
            weights[rows, columns] = weight.astype(jnp.bfloat16)
        weight = pair_weight(scale_ref, offset_ref, video_tile, last[...])
        weights[rows, pl.ds(4 * PAIR, PAIR // 2)] = weight.astype(jnp.bfloat16)

    video_sums(1, near, last_weights, weights, text, last, outs)
    columns = pl.ds(3 * PAIR, PAIR)
    edges = text_sum((near[:, columns], near_video), (weights[:, columns], video))
    columns = pl.ds(4 * PAIR, rows)
    total = text_sum((last_weights[...], near_video), (weights[:, columns], video))
    below[:rows, :] = edges[:rows].astype(jnp.bfloat16)
    above[:rows, :] = edges[rows:].astype(jnp.bfloat16)
    below[rows:, :] = (total * jnp.where(y_hi == 0, 1.0, 0.0)).astype(jnp.bfloat16)
    above[rows:, :] = (total * jnp.where(y_hi == 1, 1.0, 0.0)).astype(jnp.bfloat16)


def last_kernel(near, last_weights, far, text, last, near_video, far_video, *outs):
    video_sums(0, near, last_weights, far, text, last, outs[:4])
    for i, block in enumerate(outs[4:]):
        columns = pl.ds(i * PAIR, PAIR)
        total = text_sum((near[:, columns], near_video), (far[:, columns], far_video))
        block[...] = total.astype(jnp.bfloat16)


VMEM = pl.BlockSpec(memory_space=pltpu.VMEM)
MIB = 1024 * 1024
FLOPS = 2 * N_VIDEO * N_TEXT * PAIR * PAIR * D


def low(rows, columns=D):
    return pltpu.VMEM((rows, columns), jnp.bfloat16)


def cost(flops, transcendentals=0):
    return pl.CostEstimate(flops=flops, bytes_accessed=0, transcendentals=transcendentals)


def call(kernel, name, scalars, arrays, outs, grant, flops, transcendentals=0):
    return pl.pallas_call(
        kernel,
        out_shape=outs,
        in_specs=[SMEM] * len(scalars) + [VMEM] * len(arrays),
        out_specs=[VMEM] * len(outs),
        compiler_params=pltpu.CompilerParams(vmem_limit_bytes=grant * MIB),
        cost_estimate=cost(flops, transcendentals),
        name=name,
    )(*scalars, *arrays)


def local(footage_embeds, caption_embeds, score_scale, score_offset):
    blk = lax.axis_index("blk")
    core, y_hi = blk % 2, (blk // 2) % 2
    place = jnp.stack([core, y_hi]).astype(jnp.int32)
    scalars = [score_scale, score_offset, place]
    rows = footage_embeds.shape[0]
    v0, t0 = unit_low(footage_embeds, caption_embeds)

    a1m, a1p = move(t0, z=1), move(t0, z=-1)
    v1, tp = move(v0, y_lo=1), move(t0, y_hi=1)
    a1m, a1p, v1, tp = lax.optimization_barrier((a1m, a1p, v1, tp))
    v01 = jnp.concatenate([v0, v1])
    vm, vp = move(v01, x=1), move(v01, x=-1)
    a2m, a2p = move(a1m, z=1), move(a1p, z=-1)
    b1m, b1p = move(tp, z=1), move(tp, z=-1)
    vm, vp, b1m, b1p, a2m, a2p = lax.optimization_barrier((vm, vp, b1m, b1p, a2m, a2p))
    b2 = move_by_y_hi(jnp.where(y_hi == 1, b1p, b1m))
    v2 = move_by_core(jnp.where(core == 1, vp, vm), 1)
    own = [v01, vm, vp]
    videos = own + [move(block, core=1) for block in own]
    texts = [t0, tp, a1m, b1m, a1p, b1p, a2m, a2p]

    near_rows, far_rows = 6 * PAIR, 2 * PAIR
    near, text, near_video = call(
        near_kernel,
        "near_weights",
        scalars,
        texts + videos,
        [low(near_rows, 4 * PAIR), low(4 * PAIR), low(near_rows)],
        4,
        FLOPS * 3 // 5,
        2 * near_rows * 4 * PAIR,
    )
    v2, b2, near = lax.optimization_barrier((v2, b2, near))
    last, far, far_video, hmm, hqq, s01, sm, sp, s2 = call(
        far_kernel,
        "far_weights_and_sums",
        scalars,
        [near, text, near_video, b2, v2, move(v2, core=1)],
        [low(near_rows, PAIR // 2), low(far_rows, 4 * PAIR + PAIR // 2), low(far_rows)]
        + [low(PAIR)] * 6,
        4,
        FLOPS * 5 // 4,
        2 * far_rows * 5 * PAIR,
    )

    r2 = move(s2, core=1)
    g01, gm, gp, g2, h01, hm, hq = call(
        last_kernel,
        "own_video_and_near_text_sums",
        [],
        [near, last, far, text, b2, near_video, far_video],
        [low(PAIR)] * 7,
        4,
        FLOPS,
    )
    back = move_by_core(add(g2, r2), -1)
    hmm, hqq, back, g01, gm, gp, h01, hm, hq = lax.optimization_barrier(
        (move(hmm, z=-1), move(hqq, z=1), back, g01, gm, gp, h01, hm, hq)
    )

    up, down = move(add(hq, hqq), z=1), move(add(hm, hmm), z=-1)
    last = move(add(h01[rows:], up[rows:], down[rows:]), y_hi=1)
    text_parts = [h01, up, down, last]

    r01, rm, rp = [move(block, core=1) for block in (s01, sm, sp)]
    none = jnp.zeros((), jnp.bfloat16)
    gm = add(gm, rm, jnp.where(core == 0, back, none))
    gp = add(gp, rp, jnp.where(core == 1, back, none))
    from_p, from_m = move(gp, x=1), move(gm, x=-1)
    last = move(add(g01[rows:], r01[rows:], from_p[rows:], from_m[rows:]), y_lo=1)
    video_parts = [g01, r01, from_p, from_m, last]

    video_grad = back_rows(score_scale, footage_embeds, video_parts)
    text_grad = back_rows(score_scale, caption_embeds, text_parts)
    return (video_grad, text_grad)


def move_by_core(block, sign):
    pairs = []
    for blk in range(4 * NZ):
        step = sign if blk % 2 == 0 else -sign
        for bulk in range(2 * NX):
            to_bulk = ((bulk // 2 + step) % NX) * 2 + bulk % 2
            pairs.append((blk * 2 * NX + bulk, blk * 2 * NX + to_bulk))
    return lax.ppermute(block, AXES, pairs)


def move_by_y_hi(block):
    pairs = []
    for blk in range(4 * NZ):
        step = 1 if (blk // 2) % 2 == 0 else -1
        to_blk = ((blk // 4 + step) % NZ) * 4 + blk % 4
        for bulk in range(2 * NX):
            pairs.append((blk * 2 * NX + bulk, to_blk * 2 * NX + bulk))
    return lax.ppermute(block, AXES, pairs)


def solution(mesh):
    assert mesh.shape["blk"] == 4 * NZ and mesh.shape["bulk"] == 2 * NX
    return jax.shard_map(
        local,
        mesh=mesh,
        in_specs=(P(AXES, None), P(AXES, None), P(), P()),
        out_specs=(P(AXES, None), P(AXES, None)),
        check_vma=False,
    )
```

```python
import functools

import jax
import jax.numpy as jnp
from jax import lax
from jax.experimental import pallas as pl
from jax.experimental.pallas import tpu as pltpu
from jax.sharding import PartitionSpec as P

EPSILON = 1e-06
NZ, NX = 8, 4
AXES = ("blk", "bulk")
SMEM = pl.BlockSpec(memory_space=pltpu.SMEM)


def move(block, x=0, z=0, y_lo=0, y_hi=0, core=0):
    pairs = []
    for blk in range(4 * NZ):
        for bulk in range(2 * NX):
            to_z = (blk // 4 + z) % NZ
            to_x = (bulk // 2 + x) % NX
            to_blk = to_z * 4 + (((blk // 2) % 2) ^ y_hi) * 2 + ((blk % 2) ^ core)
            to_bulk = to_x * 2 + ((bulk % 2) ^ y_lo)
            pairs.append((blk * 2 * NX + bulk, to_blk * 2 * NX + to_bulk))
    return lax.ppermute(block, AXES, pairs)


def add(*parts):
    total = parts[0].astype(jnp.float32)
    for part in parts[1:]:
        total = total + part.astype(jnp.float32)
    return total.astype(jnp.bfloat16)


def unit_rows(embedding):
    values = embedding.astype(jnp.float32)
    inverse = lax.rsqrt(jnp.sum(values * values, axis=1, keepdims=True) + EPSILON)
    return values * inverse, inverse


def unit_kernel(video_ref, text_ref, video_out, text_out):
    text_out[...] = unit_rows(text_ref[...])[0].astype(jnp.bfloat16)
    video_out[...] = unit_rows(video_ref[...])[0].astype(jnp.bfloat16)


def unit_low(video, text):
    shape = pltpu.VMEM(video.shape, jnp.bfloat16)
    return pl.pallas_call(unit_kernel, out_shape=(shape, shape), name="unit_low")(video, text)


def back_kernel(scale_ref, embedding_ref, *refs):
    *parts, out = refs
    rows = out.shape[0]
    total = parts[0][:rows, :].astype(jnp.float32)
    for part in parts[1:]:
        total = total + part[:rows, :].astype(jnp.float32)
    grad_unit = scale_ref[0] * total
    unit, inverse = unit_rows(embedding_ref[...])
    along = jnp.sum(unit * grad_unit, axis=1, keepdims=True)
    out[...] = (grad_unit - unit * along) * inverse


def back_rows(scale, embedding, parts):
    vmem = pl.BlockSpec(memory_space=pltpu.VMEM)
    return pl.pallas_call(
        back_kernel,
        out_shape=jax.ShapeDtypeStruct(embedding.shape, jnp.float32),
        in_specs=[SMEM] + [vmem] * (1 + len(parts)),
        out_specs=vmem,
        compiler_params=pltpu.CompilerParams(vmem_limit_bytes=5 * 1024 * 1024),
        name="back_rows",
    )(scale, embedding, *parts)


PAIR, D = 256, 768
N_TEXT, N_VIDEO = 5, 8
LOG2_E = 1.4426950408889634


def put(target, blocks):
    place = 0
    for block in blocks:
        target[pl.ds(place, block.shape[0]), :] = block[...]
        place += block.shape[0]


def pair_weight(scale_ref, offset_ref, video, text):
    products = lax.dot_general(
        video, text, (((1,), (1,)), ((), ())), preferred_element_type=jnp.float32
    )
    shifted = products * (-LOG2_E * scale_ref[0]) + -LOG2_E * offset_ref[0]
    return pl.reciprocal(1.0 + jnp.exp2(shifted), approx=True)


def edge_mask(core, own):
    half = lax.broadcasted_iota(jnp.int32, (1, PAIR), 1) < PAIR // 2
    below, above = own | (core == 1), own | (core == 0)
    return jnp.where(half, jnp.where(below, 1.0, 0.0), jnp.where(above, 1.0, 0.0))


def tile_rows(step, tile):
    return pl.ds(pl.multiple_of(step * tile, tile), tile)


def near_kernel(scale_ref, offset_ref, place_ref, *refs):
    texts, videos = refs[:8], refs[8:-3]
    weights, text, video = refs[-3:]
    put(text, texts)
    put(video, videos)
    core = place_ref[0]
    tile = video.shape[0] // 2
    row = lax.broadcasted_iota(jnp.int32, (tile, PAIR), 0)
    column = lax.broadcasted_iota(jnp.int32, (tile, PAIR), 1)
    same = (row == column) & (row < PAIR // 2)

    @pl.loop(0, 2)
    def _(step):
        rows = tile_rows(step, tile)
        video_tile = video[rows, :]
        own = step == 0
        for i in range(4):
            columns = pl.ds(i * PAIR, PAIR)
            weight = pair_weight(scale_ref, offset_ref, video_tile, text[columns, :])
            if i == 0:
                weight = weight - jnp.where(same, jnp.where(own, 1.0, 0.0), 0.0)
            elif i == 3:
                weight = weight * edge_mask(core, own)
            weights[rows, columns] = weight.astype(jnp.bfloat16)


def text_sum(*pairs):
    total = None
    for weights, video in pairs:
        part = lax.dot_general(
            weights, video[...], (((0,), (0,)), ((), ())), preferred_element_type=jnp.float32
        )
        total = part if total is None else total + part
    return total


def video_sums(half, near, last_weights, far, text, last, outs):
    def dot(a, b):
        return jnp.dot(a, b[...], preferred_element_type=jnp.float32)

    for i, out in enumerate(outs[:3]):
        rows = pl.ds(half * (near.shape[0] // 2) + i * PAIR, PAIR)
        total = dot(near[rows, :], text) + dot(last_weights[rows, :], last)
        out[...] = total.astype(jnp.bfloat16)
    rows = pl.ds(half * PAIR, PAIR)
    total = dot(far[rows, : 4 * PAIR], text) + dot(far[rows, 4 * PAIR :], last)
    outs[3][...] = total.astype(jnp.bfloat16)


def far_kernel(scale_ref, offset_ref, place_ref, near, text, near_video, last, *refs):
    videos, (last_weights, weights, video, below, above, *outs) = refs[:2], refs[2:]
    put(video, videos)
    core, y_hi = place_ref[0], place_ref[1]
    near_tile, rows = near_video.shape[0] // 2, PAIR // 2

    @pl.loop(0, 2)
    def _(step):
        rows = tile_rows(step, near_tile)
        weight = pair_weight(scale_ref, offset_ref, near_video[rows, :], last[...])
        last_weights[rows, :] = weight.astype(jnp.bfloat16)
        rows = tile_rows(step, PAIR)
        video_tile = video[rows, :]
        for i in range(4):
            columns = pl.ds(i * PAIR, PAIR)
            weight = pair_weight(scale_ref, offset_ref, video_tile, text[columns, :])
            if i == 3:
                weight = weight * edge_mask(core, step == 0)
            weights[rows, columns] = weight.astype(jnp.bfloat16)
        weight = pair_weight(scale_ref, offset_ref, video_tile, last[...])
        weights[rows, pl.ds(4 * PAIR, PAIR // 2)] = weight.astype(jnp.bfloat16)

    video_sums(1, near, last_weights, weights, text, last, outs)
    columns = pl.ds(3 * PAIR, PAIR)
    edges = text_sum((near[:, columns], near_video), (weights[:, columns], video))
    columns = pl.ds(4 * PAIR, rows)
    total = text_sum((last_weights[...], near_video), (weights[:, columns], video))
    below[:rows, :] = edges[:rows].astype(jnp.bfloat16)
    above[:rows, :] = edges[rows:].astype(jnp.bfloat16)
    below[rows:, :] = (total * jnp.where(y_hi == 0, 1.0, 0.0)).astype(jnp.bfloat16)
    above[rows:, :] = (total * jnp.where(y_hi == 1, 1.0, 0.0)).astype(jnp.bfloat16)


def last_kernel(near, last_weights, far, text, last, near_video, far_video, *outs):
    video_sums(0, near, last_weights, far, text, last, outs[:4])
    for i, block in enumerate(outs[4:]):
        columns = pl.ds(i * PAIR, PAIR)
        total = text_sum((near[:, columns], near_video), (far[:, columns], far_video))
        block[...] = total.astype(jnp.bfloat16)


VMEM = pl.BlockSpec(memory_space=pltpu.VMEM)
MIB = 1024 * 1024
FLOPS = 2 * N_VIDEO * N_TEXT * PAIR * PAIR * D


def low(rows, columns=D):
    return pltpu.VMEM((rows, columns), jnp.bfloat16)


def cost(flops, transcendentals=0):
    return pl.CostEstimate(flops=flops, bytes_accessed=0, transcendentals=transcendentals)


def call(kernel, name, scalars, arrays, outs, grant, flops, transcendentals=0):
    return pl.pallas_call(
        kernel,
        out_shape=outs,
        in_specs=[SMEM] * len(scalars) + [VMEM] * len(arrays),
        out_specs=[VMEM] * len(outs),
        compiler_params=pltpu.CompilerParams(vmem_limit_bytes=grant * MIB),
        cost_estimate=cost(flops, transcendentals),
        name=name,
    )(*scalars, *arrays)


def local(footage_embeds, caption_embeds, score_scale, score_offset):
    blk = lax.axis_index("blk")
    core, y_hi = blk % 2, (blk // 2) % 2
    place = jnp.stack([core, y_hi]).astype(jnp.int32)
    scalars = [score_scale, score_offset, place]
    rows = footage_embeds.shape[0]
    v0, t0 = unit_low(footage_embeds, caption_embeds)

    a1m, a1p = move(t0, z=1), move(t0, z=-1)
    v1, tp = move(v0, y_lo=1), across_y(t0)
    a1m, a1p, v1, tp = lax.optimization_barrier((a1m, a1p, v1, tp))
    v01 = jnp.concatenate([v0, v1])
    vm, vp = move(v01, x=1), move(v01, x=-1)
    a2m, a2p = move(a1m, z=1), move(a1p, z=-1)
    b1m, b1p = move(tp, z=1), move(tp, z=-1)
    vm, vp, b1m, b1p, a2m, a2p = lax.optimization_barrier((vm, vp, b1m, b1p, a2m, a2p))
    b2 = move_by_y_hi(jnp.where(y_hi == 1, b1p, b1m))
    v2 = move_by_core(jnp.where(core == 1, vp, vm), 1)
    own = [v01, vm, vp]
    videos = own + [move(block, core=1) for block in own]
    texts = [t0, tp, a1m, b1m, a1p, b1p, a2m, a2p]

    near_rows, far_rows = 6 * PAIR, 2 * PAIR
    near, text, near_video = call(
        near_kernel,
        "near_weights",
        scalars,
        texts + videos,
        [low(near_rows, 4 * PAIR), low(4 * PAIR), low(near_rows)],
        4,
        FLOPS * 3 // 5,
        2 * near_rows * 4 * PAIR,
    )
    v2, b2, near = lax.optimization_barrier((v2, b2, near))
    last, far, far_video, hmm, hqq, s01, sm, sp, s2 = call(
        far_kernel,
        "far_weights_and_sums",
        scalars,
        [near, text, near_video, b2, v2, move(v2, core=1)],
        [low(near_rows, PAIR // 2), low(far_rows, 4 * PAIR + PAIR // 2), low(far_rows)]
        + [low(PAIR)] * 6,
        4,
        FLOPS * 5 // 4,
        2 * far_rows * 5 * PAIR,
    )

    r2 = move(s2, core=1)
    g01, gm, gp, g2, h01, hm, hq = call(
        last_kernel,
        "own_video_and_near_text_sums",
        [],
        [near, last, far, text, b2, near_video, far_video],
        [low(PAIR)] * 7,
        4,
        FLOPS,
    )
    back = move_by_core(add(g2, r2), -1)
    hmm, hqq, back, g01, gm, gp, h01, hm, hq = lax.optimization_barrier(
        (move(hmm, z=-1), move(hqq, z=1), back, g01, gm, gp, h01, hm, hq)
    )

    up, down = move(add(hq, hqq), z=1), move(add(hm, hmm), z=-1)
    last = across_y(add(h01[rows:], up[rows:], down[rows:]))
    text_parts = [h01, up, down, last]

    r01, rm, rp = [move(block, core=1) for block in (s01, sm, sp)]
    none = jnp.zeros((), jnp.bfloat16)
    gm = add(gm, rm, jnp.where(core == 0, back, none))
    gp = add(gp, rp, jnp.where(core == 1, back, none))
    from_p, from_m = move(gp, x=1), move(gm, x=-1)
    last = move(add(g01[rows:], r01[rows:], from_p[rows:], from_m[rows:]), y_lo=1)
    video_parts = [g01, r01, from_p, from_m, last]

    video_grad = back_rows(score_scale, footage_embeds, video_parts)
    text_grad = back_rows(score_scale, caption_embeds, text_parts)
    return (video_grad, text_grad)


def across_y(block):
    pairs = []
    for blk in range(4 * NZ):
        for bulk in range(2 * NX):
            y = ((blk // 2) % 2) * 2 + bulk % 2
            to_y = (y + (1 if blk % 2 == 0 else -1)) % 4
            to_blk = (blk // 4) * 4 + (to_y // 2) * 2 + blk % 2
            to_bulk = (bulk // 2) * 2 + to_y % 2
            pairs.append((blk * 2 * NX + bulk, to_blk * 2 * NX + to_bulk))
    return lax.ppermute(lax.ppermute(block, AXES, pairs), AXES, pairs)


def move_by_core(block, sign):
    pairs = []
    for blk in range(4 * NZ):
        step = sign if blk % 2 == 0 else -sign
        for bulk in range(2 * NX):
            to_bulk = ((bulk // 2 + step) % NX) * 2 + bulk % 2
            pairs.append((blk * 2 * NX + bulk, blk * 2 * NX + to_bulk))
    return lax.ppermute(block, AXES, pairs)


def move_by_y_hi(block):
    pairs = []
    for blk in range(4 * NZ):
        step = 1 if (blk // 2) % 2 == 0 else -1
        to_blk = ((blk // 4 + step) % NZ) * 4 + blk % 4
        for bulk in range(2 * NX):
            pairs.append((blk * 2 * NX + bulk, to_blk * 2 * NX + bulk))
    return lax.ppermute(block, AXES, pairs)


def solution(mesh):
    assert mesh.shape["blk"] == 4 * NZ and mesh.shape["bulk"] == 2 * NX
    return jax.shard_map(
        local,
        mesh=mesh,
        in_specs=(P(AXES, None), P(AXES, None), P(), P()),
        out_specs=(P(AXES, None), P(AXES, None)),
        check_vma=False,
    )
```

```python
import functools

import jax
import jax.numpy as jnp
from jax import lax
from jax.experimental import pallas as pl
from jax.experimental.pallas import tpu as pltpu
from jax.sharding import PartitionSpec as P

EPSILON = 1e-06
NZ, NX = 8, 4
AXES = ("blk", "bulk")
SMEM = pl.BlockSpec(memory_space=pltpu.SMEM)


def move(block, x=0, z=0, y_lo=0, y_hi=0, core=0):
    pairs = []
    for blk in range(4 * NZ):
        for bulk in range(2 * NX):
            to_z = (blk // 4 + z) % NZ
            to_x = (bulk // 2 + x) % NX
            to_blk = to_z * 4 + (((blk // 2) % 2) ^ y_hi) * 2 + ((blk % 2) ^ core)
            to_bulk = to_x * 2 + ((bulk % 2) ^ y_lo)
            pairs.append((blk * 2 * NX + bulk, to_blk * 2 * NX + to_bulk))
    return lax.ppermute(block, AXES, pairs)


def add(*parts):
    total = parts[0].astype(jnp.float32)
    for part in parts[1:]:
        total = total + part.astype(jnp.float32)
    return total.astype(jnp.bfloat16)


def unit_rows(embedding):
    values = embedding.astype(jnp.float32)
    inverse = lax.rsqrt(jnp.sum(values * values, axis=1, keepdims=True) + EPSILON)
    return values * inverse, inverse


def unit_kernel(video_ref, text_ref, video_out, text_out):
    text_out[...] = unit_rows(text_ref[...])[0].astype(jnp.bfloat16)
    video_out[...] = unit_rows(video_ref[...])[0].astype(jnp.bfloat16)


def unit_low(video, text):
    shape = pltpu.VMEM(video.shape, jnp.bfloat16)
    return pl.pallas_call(unit_kernel, out_shape=(shape, shape), name="unit_low")(video, text)


def back_kernel(scale_ref, embedding_ref, *refs):
    *parts, out = refs
    rows = out.shape[0]
    total = parts[0][:rows, :].astype(jnp.float32)
    for part in parts[1:]:
        total = total + part[:rows, :].astype(jnp.float32)
    grad_unit = scale_ref[0] * total
    unit, inverse = unit_rows(embedding_ref[...])
    along = jnp.sum(unit * grad_unit, axis=1, keepdims=True)
    out[...] = (grad_unit - unit * along) * inverse


def back_rows(scale, embedding, parts):
    vmem = pl.BlockSpec(memory_space=pltpu.VMEM)
    return pl.pallas_call(
        back_kernel,
        out_shape=jax.ShapeDtypeStruct(embedding.shape, jnp.float32),
        in_specs=[SMEM] + [vmem] * (1 + len(parts)),
        out_specs=vmem,
        compiler_params=pltpu.CompilerParams(vmem_limit_bytes=5 * 1024 * 1024),
        name="back_rows",
    )(scale, embedding, *parts)


PAIR, D = 256, 768
N_TEXT, N_VIDEO = 5, 8
LOG2_E = 1.4426950408889634


def put(target, blocks):
    place = 0
    for block in blocks:
        target[pl.ds(place, block.shape[0]), :] = block[...]
        place += block.shape[0]


def pair_weight(scale_ref, offset_ref, video, text):
    products = lax.dot_general(
        video, text, (((1,), (1,)), ((), ())), preferred_element_type=jnp.float32
    )
    shifted = products * (-LOG2_E * scale_ref[0]) + -LOG2_E * offset_ref[0]
    return pl.reciprocal(1.0 + jnp.exp2(shifted), approx=True)


def edge_mask(core, own):
    half = lax.broadcasted_iota(jnp.int32, (1, PAIR), 1) < PAIR // 2
    below, above = own | (core == 1), own | (core == 0)
    return jnp.where(half, jnp.where(below, 1.0, 0.0), jnp.where(above, 1.0, 0.0))


def tile_rows(step, tile):
    return pl.ds(pl.multiple_of(step * tile, tile), tile)


def near_kernel(scale_ref, offset_ref, place_ref, *refs):
    (t0, tp, a1m, a1p, tm, tq), videos = refs[:6], refs[6:-3]
    weights, text, video = refs[-3:]
    half = PAIR // 2
    a2m, b1m, a2p, b1p = tm[:half, :], tm[half:, :], tq[:half, :], tq[half:, :]
    put(text, [t0, tp, a1m, b1m, a1p, b1p, a2m, a2p])
    put(video, videos)
    core = place_ref[0]
    tile = video.shape[0] // 2
    row = lax.broadcasted_iota(jnp.int32, (tile, PAIR), 0)
    column = lax.broadcasted_iota(jnp.int32, (tile, PAIR), 1)
    same = (row == column) & (row < PAIR // 2)

    @pl.loop(0, 2)
    def _(step):
        rows = tile_rows(step, tile)
        video_tile = video[rows, :]
        own = step == 0
        for i in range(4):
            columns = pl.ds(i * PAIR, PAIR)
            weight = pair_weight(scale_ref, offset_ref, video_tile, text[columns, :])
            if i == 0:
                weight = weight - jnp.where(same, jnp.where(own, 1.0, 0.0), 0.0)
            elif i == 3:
                weight = weight * edge_mask(core, own)
            weights[rows, columns] = weight.astype(jnp.bfloat16)


def text_sum(*pairs):
    total = None
    for weights, video in pairs:
        part = lax.dot_general(
            weights, video[...], (((0,), (0,)), ((), ())), preferred_element_type=jnp.float32
        )
        total = part if total is None else total + part
    return total


def video_sums(half, near, last_weights, far, text, last, outs):
    def dot(a, b):
        return jnp.dot(a, b[...], preferred_element_type=jnp.float32)

    for i, out in enumerate(outs[:3]):
        rows = pl.ds(half * (near.shape[0] // 2) + i * PAIR, PAIR)
        total = dot(near[rows, :], text) + dot(last_weights[rows, :], last)
        out[...] = total.astype(jnp.bfloat16)
    rows = pl.ds(half * PAIR, PAIR)
    total = dot(far[rows, : 4 * PAIR], text) + dot(far[rows, 4 * PAIR :], last)
    outs[3][...] = total.astype(jnp.bfloat16)


def far_kernel(scale_ref, offset_ref, place_ref, near, text, near_video, last, *refs):
    videos, (last_weights, weights, video, below, above, *outs) = refs[:2], refs[2:]
    put(video, videos)
    core, y_hi = place_ref[0], place_ref[1]
    near_tile, rows = near_video.shape[0] // 2, PAIR // 2

    @pl.loop(0, 2)
    def _(step):
        rows = tile_rows(step, near_tile)
        weight = pair_weight(scale_ref, offset_ref, near_video[rows, :], last[...])
        last_weights[rows, :] = weight.astype(jnp.bfloat16)
        rows = tile_rows(step, PAIR)
        video_tile = video[rows, :]
        for i in range(4):
            columns = pl.ds(i * PAIR, PAIR)
            weight = pair_weight(scale_ref, offset_ref, video_tile, text[columns, :])
            if i == 3:
                weight = weight * edge_mask(core, step == 0)
            weights[rows, columns] = weight.astype(jnp.bfloat16)
        weight = pair_weight(scale_ref, offset_ref, video_tile, last[...])
        weights[rows, pl.ds(4 * PAIR, PAIR // 2)] = weight.astype(jnp.bfloat16)

    video_sums(1, near, last_weights, weights, text, last, outs)
    columns = pl.ds(3 * PAIR, PAIR)
    edges = text_sum((near[:, columns], near_video), (weights[:, columns], video))
    columns = pl.ds(4 * PAIR, rows)
    total = text_sum((last_weights[...], near_video), (weights[:, columns], video))
    below[:rows, :] = edges[:rows].astype(jnp.bfloat16)
    above[:rows, :] = edges[rows:].astype(jnp.bfloat16)
    below[rows:, :] = (total * jnp.where(y_hi == 0, 1.0, 0.0)).astype(jnp.bfloat16)
    above[rows:, :] = (total * jnp.where(y_hi == 1, 1.0, 0.0)).astype(jnp.bfloat16)


def last_kernel(near, last_weights, far, text, last, near_video, far_video, *outs):
    video_sums(0, near, last_weights, far, text, last, outs[:4])
    for i, block in enumerate(outs[4:]):
        columns = pl.ds(i * PAIR, PAIR)
        total = text_sum((near[:, columns], near_video), (far[:, columns], far_video))
        block[...] = total.astype(jnp.bfloat16)


VMEM = pl.BlockSpec(memory_space=pltpu.VMEM)
MIB = 1024 * 1024
FLOPS = 2 * N_VIDEO * N_TEXT * PAIR * PAIR * D


def low(rows, columns=D):
    return pltpu.VMEM((rows, columns), jnp.bfloat16)


def cost(flops, transcendentals=0):
    return pl.CostEstimate(flops=flops, bytes_accessed=0, transcendentals=transcendentals)


def call(kernel, name, scalars, arrays, outs, grant, flops, transcendentals=0):
    return pl.pallas_call(
        kernel,
        out_shape=outs,
        in_specs=[SMEM] * len(scalars) + [VMEM] * len(arrays),
        out_specs=[VMEM] * len(outs),
        compiler_params=pltpu.CompilerParams(vmem_limit_bytes=grant * MIB),
        cost_estimate=cost(flops, transcendentals),
        name=name,
    )(*scalars, *arrays)


def local(footage_embeds, caption_embeds, score_scale, score_offset):
    blk = lax.axis_index("blk")
    core, y_hi = blk % 2, (blk // 2) % 2
    place = jnp.stack([core, y_hi]).astype(jnp.int32)
    scalars = [score_scale, score_offset, place]
    rows = footage_embeds.shape[0]
    v0, t0 = unit_low(footage_embeds, caption_embeds)

    tp, v1 = move(t0, y_hi=1), move(v0, y_lo=1)
    a1m, a1p = move(t0, z=1), move(t0, z=-1)
    v1, tp, a1m, a1p = lax.optimization_barrier((v1, tp, a1m, a1p))
    v01 = jnp.concatenate([v0, v1])
    vm, vp = move(v01, x=1), move(v01, x=-1)
    tm, tq = jnp.concatenate([a1m, tp]), jnp.concatenate([a1p, tp])
    vm, vp, tm, tq = lax.optimization_barrier((vm, vp, move(tm, z=1), move(tq, z=-1)))
    b2 = move_by_y_hi(jnp.where(y_hi == 1, tq[rows:], tm[rows:]))
    v2 = move_by_core(jnp.where(core == 1, vp, vm), 1)
    own = [v01, vm, vp]
    videos = own + [move(block, core=1) for block in own]
    texts = [t0, tp, a1m, a1p, tm, tq]

    near_rows, far_rows = 6 * PAIR, 2 * PAIR
    near, text, near_video = call(
        near_kernel,
        "near_weights",
        scalars,
        texts + videos,
        [low(near_rows, 4 * PAIR), low(4 * PAIR), low(near_rows)],
        4,
        FLOPS * 3 // 5,
        2 * near_rows * 4 * PAIR,
    )
    v2, b2, near = lax.optimization_barrier((v2, b2, near))
    last, far, far_video, hmm, hqq, s01, sm, sp, s2 = call(
        far_kernel,
        "far_weights_and_sums",
        scalars,
        [near, text, near_video, b2, v2, move(v2, core=1)],
        [low(near_rows, PAIR // 2), low(far_rows, 4 * PAIR + PAIR // 2), low(far_rows)]
        + [low(PAIR)] * 6,
        4,
        FLOPS * 5 // 4,
        2 * far_rows * 5 * PAIR,
    )

    r2 = move(s2, core=1)
    g01, gm, gp, g2, h01, hm, hq = call(
        last_kernel,
        "own_video_and_near_text_sums",
        [],
        [near, last, far, text, b2, near_video, far_video],
        [low(PAIR)] * 7,
        4,
        FLOPS,
    )
    back = move_by_core(add(g2, r2), -1)
    hmm, hqq, back, g01, gm, gp, h01, hm, hq = lax.optimization_barrier(
        (move(hmm, z=-1), move(hqq, z=1), back, g01, gm, gp, h01, hm, hq)
    )

    up, down = move(add(hq, hqq), z=1), move(add(hm, hmm), z=-1)
    last = move(add(h01[rows:], up[rows:], down[rows:]), y_hi=1)
    text_parts = [h01, up, down, last]

    r01, rm, rp = [move(block, core=1) for block in (s01, sm, sp)]
    none = jnp.zeros((), jnp.bfloat16)
    gm = add(gm, rm, jnp.where(core == 0, back, none))
    gp = add(gp, rp, jnp.where(core == 1, back, none))
    from_p, from_m = move(gp, x=1), move(gm, x=-1)
    last = move(add(g01[rows:], r01[rows:], from_p[rows:], from_m[rows:]), y_lo=1)
    video_parts = [g01, r01, from_p, from_m, last]

    video_grad = back_rows(score_scale, footage_embeds, video_parts)
    text_grad = back_rows(score_scale, caption_embeds, text_parts)
    return (video_grad, text_grad)


def move_by_core(block, sign):
    pairs = []
    for blk in range(4 * NZ):
        step = sign if blk % 2 == 0 else -sign
        for bulk in range(2 * NX):
            to_bulk = ((bulk // 2 + step) % NX) * 2 + bulk % 2
            pairs.append((blk * 2 * NX + bulk, blk * 2 * NX + to_bulk))
    return lax.ppermute(block, AXES, pairs)


def move_by_y_hi(block):
    pairs = []
    for blk in range(4 * NZ):
        step = 1 if (blk // 2) % 2 == 0 else -1
        to_blk = ((blk // 4 + step) % NZ) * 4 + blk % 4
        for bulk in range(2 * NX):
            pairs.append((blk * 2 * NX + bulk, to_blk * 2 * NX + bulk))
    return lax.ppermute(block, AXES, pairs)


def solution(mesh):
    assert mesh.shape["blk"] == 4 * NZ and mesh.shape["bulk"] == 2 * NX
    return jax.shard_map(
        local,
        mesh=mesh,
        in_specs=(P(AXES, None), P(AXES, None), P(), P()),
        out_specs=(P(AXES, None), P(AXES, None)),
        check_vma=False,
    )
```
